256 devices in a mesh: row: 64 (over z_lo, x, y), col: 4 (over z_hi, core).
Axes of the slice: x: 4, y: 4, z: 8 (z_hi: 2, z_lo: 4; z = z_hi * 4 + z_lo), core: 2. Of those that a mesh axis runs over, the one named last changes fastest.
Arguments:
- charges: float32 [131072], P(('row', 'col')), may hold values from -6 to 6
- fractions: float32 [3, 131072], P(None, ('row', 'col')), may hold values from 0 to 1
- base_cells: int32 [3, 131072], P(None, ('row', 'col')), may hold values from 0 to 511, as said below
- counts: int32 [256], P(('row', 'col')), may hold values from 256 to 512, as said below
- influence: float32 [384, 256, 512], P(None, 'row', 'col'), as said below
Outputs:
- grad_charges: float32 [131072], P(('row', 'col'))
- grad_coords: float32 [3, 131072], P(None, ('row', 'col'))
The draws below stay inside these ranges and needn't reach their ends.
Inputs may be any that keep to these rules, and one draw needn't show every extreme that they name: Atom slot i lies on device i // 512, numbered row index times the size of col plus col index; on the device with row index r and col index c, base_cells[0] lies in [r * 6, (r + 1) * 6), base_cells[1] in [c * 64, (c + 1) * 64), base_cells[2] anywhere. `counts`: slots from a device's count up to 512 hold no atom; some device is full in every draw. `influence`: nonnegative, zero at the zero wave vector.
All inputs are finite; a program needn't handle non-finite values.
Results may differ from the reference program's by a relative error of at most 0.0003.
Values sent between devices are 32-bit elements; how exact they have to be, the bound alone decides.
A program may use at most 64 MiB of HBM per device.

```python
import math
import jax
import jax.numpy as jnp
from jax import lax

KX = 384
KY = 256
KZ = 512
ORDER = 6
SLOTS = 512
CX = 6
CY = 64
ATOMS = 131072
N_COL = 4
DEVICES = 256


screening = 0.15


spline_knots = (1.0 / 120.0, 26.0 / 120.0, 66.0 / 120.0, 26.0 / 120.0, 1.0 / 120.0)


def draw_base_cells(key, part):
    key = jax.random.fold_in(key, 11)
    key_first, key_second, key_third = jax.random.split(key, 3)
    slot_index = jnp.arange(ATOMS, dtype=jnp.int32)
    device = slot_index // SLOTS
    row_index = device // N_COL
    col_index = device % N_COL
    first = row_index * CX + jax.random.randint(key_first, (ATOMS,), 0, CX)
    second = col_index * CY + jax.random.randint(key_second, (ATOMS,), 0, CY)
    third = jax.random.randint(key_third, (ATOMS,), 0, KZ)
    return jnp.stack([first, second, third]).astype(jnp.int32)


def draw_counts(key, part):
    key = jax.random.fold_in(key, 12)
    key_fill, key_full = jax.random.split(key)
    filled = jax.random.randint(key_fill, (DEVICES,), SLOTS // 2, SLOTS + 1)
    full_device = jax.random.randint(key_full, (), 0, DEVICES)
    return jnp.where(jnp.arange(DEVICES) == full_device, SLOTS, filled).astype(jnp.int32)


def wave_squared(length):
    index = jnp.arange(length, dtype=jnp.int32)
    wrapped = jnp.where(index <= length // 2, index, index - length).astype(jnp.float32)
    return (wrapped / length) ** 2


def spline_module(length):
    index = jnp.arange(length, dtype=jnp.int32)
    real_part = jnp.zeros((length,), jnp.float32)
    imag_part = jnp.zeros((length,), jnp.float32)
    for position in range(5):
        angles = (index * position % length).astype(jnp.float32) * (2.0 * math.pi / length)
        real_part = real_part + spline_knots[position] * jnp.cos(angles)
        imag_part = imag_part + spline_knots[position] * jnp.sin(angles)
    return 1.0 / (real_part * real_part + imag_part * imag_part)


def draw_influence(key, part):
    key = jax.random.fold_in(key, 13)
    squared = wave_squared(KX)[:, None, None] + wave_squared(KY)[None, :, None] + wave_squared(KZ)[None, None, :]
    smooth = jnp.exp(-math.pi ** 2 * squared) / (squared + screening ** 2)
    module = spline_module(KX)[:, None, None] * spline_module(KY)[None, :, None] * spline_module(KZ)[None, None, :]
    rough = jnp.exp(jax.random.uniform(key, (KX, KY, KZ), jnp.float32, math.log(0.5), math.log(2.0)))
    scaled = smooth * module * rough / math.sqrt(32.0 * KX * KY * KZ * ATOMS)
    return jnp.where(squared > 0, scaled, 0.0).astype(jnp.float32)


def block_scale(stream_key, dims, cuts, low, top_value):
    def one(dim, parts):
        steps = jax.random.uniform(jax.random.fold_in(jax.random.fold_in(stream_key, 6), dim), (parts,), jnp.float32, low / len(cuts), top_value / len(cuts))
        return jnp.repeat(jnp.exp(steps), dims[dim] // parts).reshape((-1,) + (1,) * (len(dims) - dim - 1))

    loudness = one(*cuts[0])
    for cut in cuts[1:]:
        loudness = loudness * one(*cut)
    return loudness


def scatter_about(stream_key, shape, width, reach, cuts=(), held_as=jnp.bfloat16):
    drawn = jax.random.normal(stream_key, shape, jnp.float32) * width
    if len(cuts) > 0:
        drawn = block_scale(stream_key, shape, cuts, -0.22, 0.18) * drawn
    return jnp.clip(drawn, min=-reach, max=reach).astype(held_as)


def setup_inputs(seed: int = 0) -> dict:
    seeds = jax.random.split(jax.random.key(seed), 6)
    charges = scatter_about(seeds[0], (ATOMS,), 1.0, 6.0, ((0, 256),), jnp.float32)
    fractions = jnp.clip(1.0 * jax.random.uniform(seeds[1], (3, ATOMS), jnp.float32) ** block_scale(seeds[1], (3, ATOMS), ((1, 256),), -0.2, 0.2), 0.0, 1.0)
    base_cells = draw_base_cells(jax.random.fold_in(seeds[5], 71), 0)
    counts = draw_counts(jax.random.fold_in(seeds[5], 71), 0)
    influence = draw_influence(jax.random.fold_in(seeds[5], 71), 0)
    return {"charges": charges, "fractions": fractions, "base_cells": base_cells, "counts": counts, "influence": influence}


def spline_tables(fraction):
    previous = [fraction, 1.0 - fraction]
    fifth_order = previous
    for degree in range(3, 7):
        current = []
        for position in range(degree):
            summed = jnp.zeros_like(fraction)
            if position < degree - 1:
                summed = summed + (fraction + position) * previous[position]
            if position >= 1:
                summed = summed + (degree - fraction - position) * previous[position - 1]
            current.append(summed / (degree - 1))
        fifth_order = previous
        previous = current
    slopes = []
    for position in range(6):
        gradient = jnp.zeros_like(fraction)
        if position < 5:
            gradient = gradient + fifth_order[position]
        if position >= 1:
            gradient = gradient - fifth_order[position - 1]
        slopes.append(gradient)
    return jnp.stack(previous[::-1]), jnp.stack(slopes[::-1])


def hartley_axis(field, axis):
    transformed = jnp.fft.fft(field, axis=axis)
    return (transformed.real - transformed.imag).astype(jnp.float32)


def hartley_all(field):
    for axis in range(3):
        field = hartley_axis(field, axis)
    return field


def reference(charges, fractions, base_cells, counts, influence):
    total = charges.shape[0]
    slot_index = jnp.arange(total, dtype=jnp.int32)
    device = slot_index // SLOTS
    live_slot = (slot_index % SLOTS) < counts[device]
    weight = jnp.where(live_slot, charges, jnp.float32(0.0))
    spline, spline_slope = spline_tables(fractions)
    offsets = jnp.arange(ORDER, dtype=jnp.int32)
    cell_x = (base_cells[0][None, :] + offsets[:, None]) % KX
    cell_y = (base_cells[1][None, :] + offsets[:, None]) % KY
    cell_z = (base_cells[2][None, :] + offsets[:, None]) % KZ
    charge_grid = jnp.zeros((KX * KY * KZ,), jnp.float32)
    index_list = []
    for offset_x in range(ORDER):
        cell_index = (cell_x[offset_x][None, None, :] * KY + cell_y[:, None, :]) * KZ + cell_z[None, :, :]
        index_list.append(cell_index)
        values = weight * spline[offset_x, 0] * spline[:, 1][:, None, :] * spline[:, 2][None, :, :]
        charge_grid = charge_grid.at[cell_index].add(values)
    spectrum = hartley_all(charge_grid.reshape(KX, KY, KZ))
    potential = hartley_all(influence * spectrum).reshape(-1)
    high = lax.Precision.HIGHEST
    grad_charge = jnp.zeros((total,), jnp.float32)
    grad_first = jnp.zeros((total,), jnp.float32)
    grad_second = jnp.zeros((total,), jnp.float32)
    grad_third = jnp.zeros((total,), jnp.float32)
    for offset_x in range(ORDER):
        patches = potential[index_list[offset_x]]
        inner = jnp.einsum('bcs,bs,cs->s', patches, spline[:, 1], spline[:, 2], precision=high)
        along_y = jnp.einsum('bcs,bs,cs->s', patches, spline_slope[:, 1], spline[:, 2], precision=high)
        along_z = jnp.einsum('bcs,bs,cs->s', patches, spline[:, 1], spline_slope[:, 2], precision=high)
        grad_charge = grad_charge + spline[offset_x, 0] * inner
        grad_first = grad_first + spline_slope[offset_x, 0] * inner
        grad_second = grad_second + spline[offset_x, 0] * along_y
        grad_third = grad_third + spline[offset_x, 0] * along_z
    grad_charges = jnp.where(live_slot, grad_charge, jnp.float32(0.0))
    grad_coords = weight[None, :] * jnp.stack([grad_first, grad_second, grad_third])
    return grad_charges, grad_coords
```

```python
import functools
import math

import jax
import jax.numpy as jnp
import ml_dtypes
import numpy as np
from jax import lax
from jax.experimental import pallas as pl
from jax.experimental.pallas import tpu as pltpu
from jax.sharding import PartitionSpec as P

KX = 384
KY = 256
KZ = 512
ORDER = 6
SLOTS = 512
ROWS = 64
COLS = 4
CX = KX // ROWS
CY = KY // COLS
CZ = KZ // COLS
PATCH_Y = 72
FINE = 8
COARSE = KZ // FINE
FAN = 2 * FINE
VMEM_LIMIT = 50 * 1024 * 1024

HIGH_TYPE = jnp.bfloat16
FLOAT = jnp.float32


def split_table(table):
    high = table.astype(np.float32).astype(ml_dtypes.bfloat16)
    low = (table - high.astype(np.float64)).astype(np.float32).astype(ml_dtypes.bfloat16)
    return high, low


def cas(product, length):
    angles = (product % length) * (2.0 * math.pi / length)
    return np.cos(angles) + np.sin(angles)


def make_tables():
    kx = np.arange(KX)
    table_x = np.stack(split_table(cas(kx[:, None] * kx[None, :], KX)))
    ky = np.arange(KY)
    y = np.arange(KY + 8)
    table_y = np.stack(split_table(cas(y[:, None] * ky[None, :], KY)))
    kz = np.arange(KZ)
    coarse = (kz[:, None] * np.arange(COARSE)[None, :] * FINE % KZ) * (2.0 * math.pi / KZ)
    fine = kz[:, None] * np.arange(FAN)[None, :]
    table_z = np.zeros((COLS, 4 * CZ, 3 * FAN + 2 * COARSE), ml_dtypes.bfloat16)
    for place, values in ((0, np.cos(coarse)), (1, np.sin(coarse))):
        high, low = split_table(values)
        rows = slice(place * CZ, (place + 1) * CZ)
        table_z[:, rows, 3 * FAN : 3 * FAN + COARSE] = high.reshape(COLS, CZ, COARSE)
        table_z[:, rows, 3 * FAN + COARSE :] = low.reshape(COLS, CZ, COARSE)
    for place, values in ((2, cas(fine, KZ)), (3, cas(-fine, KZ))):
        high, low = split_table(values)
        rows = slice(place * CZ, (place + 1) * CZ)
        table_z[:, rows, :FAN] = high.reshape(COLS, CZ, FAN)
        table_z[:, rows, FAN : 2 * FAN] = high.reshape(COLS, CZ, FAN)
        table_z[:, rows, 2 * FAN : 3 * FAN] = low.reshape(COLS, CZ, FAN)
    return table_x, table_y, table_z


def spline_tables(fraction):
    previous = [fraction, 1.0 - fraction]
    fifth_order = previous
    for degree in range(3, 7):
        current = []
        for position in range(degree):
            summed = None
            if position < degree - 1:
                summed = (fraction + position) * previous[position]
            if position >= 1:
                second = (degree - fraction - position) * previous[position - 1]
                summed = second if summed is None else summed + second
            current.append(summed * (1.0 / (degree - 1)))
        fifth_order = previous
        previous = current
    slopes = []
    for position in range(6):
        if position == 0:
            slopes.append(fifth_order[0])
        elif position == 5:
            slopes.append(-fifth_order[4])
        else:
            slopes.append(fifth_order[position] - fifth_order[position - 1])
    return previous[::-1], slopes[::-1]


def split(value):
    high = value.astype(HIGH_TYPE)
    return high, (value - high.astype(FLOAT)).astype(HIGH_TYPE)


def dot(left, right, transposed=False):
    dims = (((1,), (1 if transposed else 0,)), ((), ()))
    return lax.dot_general(left, right, dims, preferred_element_type=FLOAT)


def dot3(left_high, left_low, right_high, right_low):
    return (
        dot(left_high, right_high) + dot(left_high, right_low) + dot(left_low, right_high)
    )


def dense(base, weights, rows):
    distance = lax.broadcasted_iota(jnp.int32, (rows, SLOTS), 0).astype(FLOAT) - base
    total = jnp.zeros((rows, SLOTS), FLOAT)
    for offset in range(ORDER):
        total = jnp.where(distance == offset, weights[offset], total)
    return total


def spread_kernel(atoms_ref, table_z_ref, table_y_ref, out_ref, z_ref, spline_ref, acc_ref):
    col = lax.axis_index("col")
    for dim in range(3):
        values, slopes = spline_tables(atoms_ref[:, 1 + dim, :])
        for offset in range(ORDER):
            spline_ref[dim, offset] = values[offset]
            spline_ref[dim, ORDER + offset] = slopes[offset]
    acc_ref[...] = jnp.zeros(acc_ref.shape, FLOAT)

    def block(index, carry):
        part = lax.rem(index, COLS)
        weight = atoms_ref[index, 0:1, :]
        base_x = atoms_ref[index, 4:5, :]
        base_y = atoms_ref[index, 5:6, :]
        base_z = atoms_ref[index, 6:7, :]

        def row(dim, place):
            return spline_ref[dim, place, pl.ds(index, 1), :]

        dense_x = weight * dense(base_x, [row(0, a) for a in range(ORDER)], 8)
        dense_y = dense(base_y, [row(1, a) for a in range(ORDER)], PATCH_Y)
        coarse = jnp.floor(base_z * (1.0 / FINE))
        rest = base_z - coarse * FINE
        hit = lax.broadcasted_iota(jnp.int32, (COARSE, SLOTS), 0).astype(FLOAT) == coarse
        hit = jnp.where(hit, 1.0, 0.0).astype(HIGH_TYPE)
        fine_high, fine_low = split(dense(rest, [row(2, a) for a in range(ORDER)], FAN))
        slope_high, slope_low = split(dense(rest, [row(2, ORDER + a) for a in range(ORDER)], FAN))
        table = table_z_ref[col]
        joined = jnp.concatenate([fine_high, fine_low, fine_high, hit, hit], axis=0)
        parts = dot(table, joined)
        joined_slope = jnp.concatenate([slope_high, slope_low, slope_high], axis=0)
        parts_slope = dot(table[2 * CZ :, : 3 * FAN], joined_slope)
        cosine, sine = parts[:CZ], parts[CZ : 2 * CZ]
        wave = cosine * parts[2 * CZ : 3 * CZ] + sine * parts[3 * CZ :]
        wave_slope = cosine * parts_slope[:CZ] + sine * parts_slope[CZ:]
        wave_high, wave_low = split(wave)
        slope_high, slope_low = split(wave_slope)
        z_ref[index, 0:CZ] = wave_high
        z_ref[index, CZ : 2 * CZ] = wave_low
        z_ref[index, 2 * CZ : 3 * CZ] = slope_high
        z_ref[index, 3 * CZ :] = slope_low
        patch = jnp.concatenate([dense_x[x : x + 1] * dense_y for x in range(CX)], axis=0)
        patch_high, patch_low = split(patch)
        first = dot(patch_high, jnp.concatenate([wave_high, wave_low], axis=0), True)
        summed = first[:, :CZ] + first[:, CZ:] + dot(patch_low, wave_high, True)
        rows = pl.ds(pl.multiple_of(part * CY, CY), PATCH_Y)
        for x in range(CX):
            acc_ref[x, rows, :] += summed[x * PATCH_Y : (x + 1) * PATCH_Y]
        return carry

    lax.fori_loop(0, 2 * COLS, block, 0)
    for x in range(CX):
        acc_ref[x, 0:8, :] += acc_ref[x, KY : KY + 8, :]
    for pair in range(CX // 2):
        field = jnp.concatenate([acc_ref[2 * pair, :KY], acc_ref[2 * pair + 1, :KY]], axis=1)
        high, low = split(field)
        result = dot3(table_y_ref[0, :KY], table_y_ref[1, :KY], high, low)
        out_ref[2 * pair] = result[:, :CZ]
        out_ref[2 * pair + 1] = result[:, CZ:]


def middle_kernel(field_ref, influence_ref, table_ref, out_ref):
    width = KY // ROWS
    field = jnp.concatenate([field_ref[pl.ds(j, KX, stride=width), :] for j in range(width)], axis=1)
    weight = jnp.concatenate(
        [influence_ref[pl.ds(j, KX, stride=width), :] for j in range(width)], axis=1
    )
    high, low = split(field)
    spectrum = weight * dot3(table_ref[0], table_ref[1], high, low)
    high, low = split(spectrum)
    result = dot3(table_ref[0], table_ref[1], high, low)
    for j in range(width):
        out_ref[pl.ds(j, KX, stride=width), :] = result[:, j * CZ : (j + 1) * CZ]


def gather_kernel(field_ref, atoms_ref, z_ref, spline_ref, table_y_ref, out_ref, real_ref):
    for pair in range(CX // 2):
        field = jnp.concatenate([field_ref[2 * pair], field_ref[2 * pair + 1]], axis=1)
        high, low = split(field)
        result = dot3(table_y_ref[0], table_y_ref[1], high, low)
        real_ref[2 * pair] = result[:, :CZ]
        real_ref[2 * pair + 1] = result[:, CZ:]

    def block(index, carry):
        part = lax.rem(index, COLS)
        base_x = atoms_ref[index, 4:5, :]
        base_y = atoms_ref[index, 5:6, :]

        def row(dim, place):
            return spline_ref[dim, place, pl.ds(index, 1), :]

        dense_x = dense(base_x, [row(0, a) for a in range(ORDER)], 8)
        slope_x = dense(base_x, [row(0, ORDER + a) for a in range(ORDER)], 8)
        dense_y = dense(base_y, [row(1, a) for a in range(ORDER)], PATCH_Y)
        slope_y = dense(base_y, [row(1, ORDER + a) for a in range(ORDER)], PATCH_Y)
        rows = pl.ds(pl.multiple_of(part * CY, CY), PATCH_Y)
        patch = jnp.concatenate([real_ref[x, rows, :] for x in range(CX)], axis=0)
        high, low = split(patch)
        both = jnp.concatenate([high, low], axis=1)

        def contract(place):
            wave_high = z_ref[index, place * CZ : (place + 1) * CZ]
            wave_low = z_ref[index, (place + 1) * CZ : (place + 2) * CZ]
            return dot(both, jnp.concatenate([wave_high, wave_high], axis=0)) + dot(high, wave_low)

        plain = contract(0)
        third = contract(2)
        charge = first = second = last = 0.0
        for x in range(CX):
            here = plain[x * PATCH_Y : (x + 1) * PATCH_Y]
            there = third[x * PATCH_Y : (x + 1) * PATCH_Y]
            inner = jnp.sum(dense_y * here, axis=0, keepdims=True)
            along_y = jnp.sum(slope_y * here, axis=0, keepdims=True)
            along_z = jnp.sum(dense_y * there, axis=0, keepdims=True)
            charge = charge + dense_x[x : x + 1] * inner
            first = first + slope_x[x : x + 1] * inner
            second = second + dense_x[x : x + 1] * along_y
            last = last + dense_x[x : x + 1] * along_z
        out_ref[index, 0:1] = charge
        out_ref[index, 1:2] = first
        out_ref[index, 2:3] = second
        out_ref[index, 3:4] = last
        return carry

    lax.fori_loop(0, 2 * COLS, block, 0)


def call(kernel, outs, scratch=()):
    return pl.pallas_call(
        kernel,
        out_shape=outs,
        scratch_shapes=list(scratch),
        compiler_params=pltpu.CompilerParams(vmem_limit_bytes=VMEM_LIMIT),
    )


def shape(dims, kind=FLOAT):
    return jax.ShapeDtypeStruct(dims, kind)


def per_device(charges, fractions, base_cells, counts, influence):
    table_x, table_y, table_z = (jnp.asarray(t) for t in make_tables())
    row_at = lax.axis_index("row")
    col_at = lax.axis_index("col")
    live_slot = jnp.arange(SLOTS, dtype=jnp.int32) < counts[0]
    weight = jnp.where(live_slot, charges, jnp.float32(0.0))
    offsets = jnp.stack([row_at * CX, col_at * CY, jnp.zeros((), jnp.int32)])
    local = (base_cells - offsets[:, None]).astype(FLOAT)
    pack = jnp.concatenate(
        [weight[None], fractions, local, jnp.zeros((1, SLOTS), FLOAT)], axis=0
    )
    shared = lax.all_gather(pack, "col")
    forward = [(source, (source + 1) % ROWS) for source in range(ROWS)]
    behind = lax.ppermute(shared, "row", forward)
    behind = behind.at[:, 4].add(-float(CX))
    atoms = jnp.concatenate([shared, behind], axis=0)
    blocks = 2 * COLS
    spectrum, waves, splines = call(
        spread_kernel,
        (
            shape((CX, KY, CZ)),
            shape((blocks, 4 * CZ, SLOTS), HIGH_TYPE),
            shape((3, 2 * ORDER, blocks, SLOTS)),
        ),
        [pltpu.VMEM((CX, KY + 8, CZ), FLOAT)],
    )(atoms, table_z, table_y)
    turned = lax.all_to_all(spectrum, "row", split_axis=1, concat_axis=0, tiled=True)
    width = KY // ROWS
    field = call(middle_kernel, shape((KX * width, CZ)))(
        turned.reshape(KX * width, CZ), influence.reshape(KX * width, CZ), table_x
    )
    returned = lax.all_to_all(
        field.reshape(KX, width, CZ), "row", split_axis=0, concat_axis=1, tiled=True
    )
    partial = call(
        gather_kernel,
        shape((blocks, 4, SLOTS)),
        [pltpu.VMEM((CX, KY + 8, CZ), FLOAT)],
    )(returned, atoms, waves, splines, table_y)
    backward = [(source, (source - 1) % ROWS) for source in range(ROWS)]
    mine = partial[:COLS] + lax.ppermute(partial[COLS:], "row", backward)
    total = lax.psum_scatter(mine, "col", scatter_dimension=0, tiled=False)
    grad_charges = jnp.where(live_slot, total[0], jnp.float32(0.0))
    grad_coords = weight[None, :] * total[1:]
    return (grad_charges, grad_coords)


def solution(mesh):
    return jax.shard_map(
        per_device,
        mesh=mesh,
        in_specs=(
            P(("row", "col")),
            P(None, ("row", "col")),
            P(None, ("row", "col")),
            P(("row", "col")),
            P(None, "row", "col"),
        ),
        out_specs=(P(("row", "col")), P(None, ("row", "col"))),
        check_vma=False,
    )
```

```python
import math

import jax
import jax.numpy as jnp
import ml_dtypes
import numpy as np
from jax import lax
from jax.experimental import pallas as pl
from jax.experimental.pallas import tpu as pltpu
from jax.sharding import PartitionSpec as P

KX = 384
KY = 256
KZ = 512
ORDER = 6
SLOTS = 512
ROWS = 64
COLS = 4
CX = KX // ROWS
CY = KY // COLS
CZ = KZ // COLS
PATCH_Y = 72
FINE = 8
COARSE = KZ // FINE
FAN = 2 * FINE
VMEM_LIMIT = 50 * 1024 * 1024
SPREAD_GROUPS = 3
GATHER_GROUPS = 3
MESH = pl.DeviceIdType.MESH

HIGH_TYPE = jnp.bfloat16
FLOAT = jnp.float32


def split_table(table):
    high = table.astype(np.float32).astype(ml_dtypes.bfloat16)
    low = (table - high.astype(np.float64)).astype(np.float32).astype(ml_dtypes.bfloat16)
    return high, low


def cas(product, length):
    angles = (product % length) * (2.0 * math.pi / length)
    return np.cos(angles) + np.sin(angles)


def make_tables():
    kx = np.arange(KX)
    table_x = np.stack(split_table(cas(kx[:, None] * kx[None, :], KX)))
    ky = np.arange(KY)
    y = np.arange(KY + 8)
    table_y = np.stack(split_table(cas(y[:, None] * ky[None, :], KY)))
    kz = np.arange(KZ)
    coarse = (kz[:, None] * np.arange(COARSE)[None, :] * FINE % KZ) * (2.0 * math.pi / KZ)
    fine = kz[:, None] * np.arange(FAN)[None, :]
    table_z = np.zeros((COLS, 4 * CZ, 3 * FAN + 2 * COARSE), ml_dtypes.bfloat16)
    for place, values in ((0, np.cos(coarse)), (1, np.sin(coarse))):
        high, low = split_table(values)
        rows = slice(place * CZ, (place + 1) * CZ)
        table_z[:, rows, 3 * FAN : 3 * FAN + COARSE] = high.reshape(COLS, CZ, COARSE)
        table_z[:, rows, 3 * FAN + COARSE :] = low.reshape(COLS, CZ, COARSE)
    for place, values in ((2, cas(fine, KZ)), (3, cas(-fine, KZ))):
        high, low = split_table(values)
        rows = slice(place * CZ, (place + 1) * CZ)
        table_z[:, rows, :FAN] = high.reshape(COLS, CZ, FAN)
        table_z[:, rows, FAN : 2 * FAN] = high.reshape(COLS, CZ, FAN)
        table_z[:, rows, 2 * FAN : 3 * FAN] = low.reshape(COLS, CZ, FAN)
    return table_x, table_y, table_z


def spline_tables(fraction):
    previous = [fraction, 1.0 - fraction]
    fifth_order = previous
    for degree in range(3, 7):
        current = []
        for position in range(degree):
            summed = None
            if position < degree - 1:
                summed = (fraction + position) * previous[position]
            if position >= 1:
                second = (degree - fraction - position) * previous[position - 1]
                summed = second if summed is None else summed + second
            current.append(summed * (1.0 / (degree - 1)))
        fifth_order = previous
        previous = current
    slopes = []
    for position in range(6):
        if position == 0:
            slopes.append(fifth_order[0])
        elif position == 5:
            slopes.append(-fifth_order[4])
        else:
            slopes.append(fifth_order[position] - fifth_order[position - 1])
    return previous[::-1], slopes[::-1]


def split(value):
    high = value.astype(HIGH_TYPE)
    return high, (value - high.astype(FLOAT)).astype(HIGH_TYPE)


def dot(left, right, transposed=False):
    dims = (((1,), (1 if transposed else 0,)), ((), ()))
    return lax.dot_general(left, right, dims, preferred_element_type=FLOAT)


def dot3(left_high, left_low, right_high, right_low):
    return (
        dot(left_high, right_high) + dot(left_high, right_low) + dot(left_low, right_high)
    )


def dense(base, weights, rows):
    distance = lax.broadcasted_iota(jnp.int32, (rows, SLOTS), 0).astype(FLOAT) - base
    total = jnp.zeros((rows, SLOTS), FLOAT)
    for offset in range(ORDER):
        total = jnp.where(distance == offset, weights[offset], total)
    return total


def kernel(
    charges_ref,
    fractions_ref,
    cells_ref,
    counts_ref,
    influence_hbm,
    table_x_hbm,
    table_y_hbm,
    table_z_hbm,
    out_charges_ref,
    out_coords_ref,
    influence_ref,
    table_x_ref,
    table_y_ref,
    table_z_ref,
    atoms_ref,
    spline_ref,
    dense_x_ref,
    dense_y_ref,
    z_ref,
    acc_ref,
    send_ref,
    turned_ref,
    back_ref,
    returned_ref,
    partial_ref,
    arrived_ref,
    local_sems,
    send_sems,
    atoms_sem,
    turned_sem,
    returned_sems,
    arrived_sem,
):
    row = lax.axis_index("row")
    col = lax.axis_index("col")
    row_after = lax.rem(row + 1, ROWS)
    row_before = lax.rem(row + ROWS - 1, ROWS)
    width = KY // ROWS
    blocks = 2 * COLS

    barrier = pltpu.get_barrier_semaphore()

    def greet(device_row, device_col):
        pl.semaphore_signal(
            barrier, inc=1, device_id=(device_row, device_col), device_id_type=MESH
        )

    for step in range(1, COLS):
        other = lax.rem(col + step, COLS)
        greet(row, other)
        greet(row_after, other)
        greet(row_before, other)

    @pl.loop(1, ROWS)
    def _(step):
        greet(lax.rem(row + step, ROWS), col)

    fetches = [
        pltpu.make_async_copy(table_z_hbm.at[col], table_z_ref, local_sems.at[0]),
        pltpu.make_async_copy(table_y_hbm, table_y_ref, local_sems.at[1]),
        pltpu.make_async_copy(table_x_hbm, table_x_ref, local_sems.at[2]),
        pltpu.make_async_copy(influence_hbm, influence_ref, local_sems.at[3]),
    ]
    for fetch in fetches:
        fetch.start()

    slot = lax.broadcasted_iota(jnp.int32, (1, SLOTS), 1)
    live = slot < counts_ref[0]
    weight = jnp.where(live, charges_ref[...], 0.0)
    atoms_ref[col, 0:1, :] = weight
    atoms_ref[col, 1:4, :] = fractions_ref[...]
    cells = cells_ref[...]
    atoms_ref[col, 4:5, :] = (cells[0:1] - row * CX).astype(FLOAT)
    atoms_ref[col, 5:6, :] = (cells[1:2] - col * CY).astype(FLOAT)
    atoms_ref[col, 6:7, :] = cells[2:3].astype(FLOAT)
    atoms_ref[col, 7:8, :] = weight

    pl.semaphore_wait(barrier, ROWS - 1 + 3 * (COLS - 1))

    def remote(source, target, send_sem, recv_sem, device_row, device_col):
        return pltpu.make_async_remote_copy(
            src_ref=source,
            dst_ref=target,
            send_sem=send_sem,
            recv_sem=recv_sem,
            device_id=(device_row, device_col),
            device_id_type=MESH,
        )

    for step in range(1, COLS):
        other = lax.rem(col + step, COLS)
        remote(
            atoms_ref.at[col], atoms_ref.at[col], send_sems.at[0], atoms_sem, row, other
        ).start()
    for step in range(COLS):
        other = lax.rem(col + step, COLS)
        remote(
            atoms_ref.at[col],
            atoms_ref.at[COLS + col],
            send_sems.at[0],
            atoms_sem,
            row_after,
            other,
        ).start()
    remote(
        atoms_ref.at[0 : blocks - 1],
        atoms_ref.at[0 : blocks - 1],
        send_sems.at[0],
        atoms_sem,
        row_after,
        col,
    ).wait()

    for dim in range(3):
        values, slopes = spline_tables(atoms_ref[:, 1 + dim, :])
        for offset in range(ORDER):
            spline_ref[dim, offset] = values[offset]
            spline_ref[dim, ORDER + offset] = slopes[offset]
    fetches[0].wait()

    @pl.loop(0, blocks)
    def _(index):
        shift = (CX * (index // COLS)).astype(FLOAT)
        weight = atoms_ref[index, 0:1, :]
        base_x = atoms_ref[index, 4:5, :] - shift
        base_y = atoms_ref[index, 5:6, :]
        base_z = atoms_ref[index, 6:7, :]

        def rows(dim, place):
            return [
                spline_ref[dim, place + offset, pl.ds(index, 1), :] for offset in range(ORDER)
            ]

        plain_x = dense(base_x, rows(0, 0), 8)
        dense_x_ref[index, 0] = plain_x
        dense_x_ref[index, 1] = dense(base_x, rows(0, ORDER), 8)
        dense_x_ref[index, 2] = weight * plain_x
        dense_y_ref[index, 0] = dense(base_y, rows(1, 0), PATCH_Y)
        dense_y_ref[index, 1] = dense(base_y, rows(1, ORDER), PATCH_Y)
        coarse = jnp.floor(base_z * (1.0 / FINE))
        rest = base_z - coarse * FINE
        hit = lax.broadcasted_iota(jnp.int32, (COARSE, SLOTS), 0).astype(FLOAT) == coarse
        hit = jnp.where(hit, 1.0, 0.0).astype(HIGH_TYPE)
        fine_high, fine_low = split(dense(rest, rows(2, 0), FAN))
        slope_high, slope_low = split(dense(rest, rows(2, ORDER), FAN))
        joined = jnp.concatenate([fine_high, fine_low, fine_high, hit, hit], axis=0)
        parts = dot(table_z_ref[...], joined)
        joined_slope = jnp.concatenate([slope_high, slope_low, slope_high], axis=0)
        parts_slope = dot(table_z_ref[2 * CZ :, : 3 * FAN], joined_slope)
        cosine, sine = parts[:CZ], parts[CZ : 2 * CZ]
        wave = cosine * parts[2 * CZ : 3 * CZ] + sine * parts[3 * CZ :]
        wave_slope = cosine * parts_slope[:CZ] + sine * parts_slope[CZ:]
        wave_high, wave_low = split(wave)
        slope_high, slope_low = split(wave_slope)
        z_ref[index, 0:CZ] = wave_high
        z_ref[index, CZ : 2 * CZ] = wave_low
        z_ref[index, 2 * CZ : 3 * CZ] = slope_high
        z_ref[index, 3 * CZ :] = slope_low

    send_flat = send_ref.reshape(CX, KY, CZ)
    for group in range(SPREAD_GROUPS):
        count = CX // SPREAD_GROUPS
        first_x = group * count
        acc_ref[0:count] = jnp.zeros((count, KY + 8, CZ), FLOAT)

        @pl.loop(0, blocks)
        def _(index):
            part = lax.rem(index, COLS)
            plain_y = dense_y_ref[index, 0]
            patch = jnp.concatenate(
                [dense_x_ref[index, 2, x : x + 1, :] * plain_y for x in range(first_x, first_x + count)],
                axis=0,
            )
            high, low = split(patch)
            both = dot(high, z_ref[index, 0 : 2 * CZ], True)
            summed = both[:, :CZ] + both[:, CZ:] + dot(low, z_ref[index, 0:CZ], True)
            rows = pl.ds(pl.multiple_of(part * CY, CY), PATCH_Y)
            for x in range(count):
                acc_ref[x, rows, :] += summed[x * PATCH_Y : (x + 1) * PATCH_Y]

        if group == 0:
            fetches[1].wait()
        for x in range(count):
            acc_ref[x, 0:8, :] += acc_ref[x, KY : KY + 8, :]
        field = jnp.concatenate([acc_ref[x, :KY] for x in range(count)], axis=1)
        high, low = split(field)
        result = dot3(table_y_ref[0, :KY], table_y_ref[1, :KY], high, low)
        for x in range(count):
            send_flat[first_x + x] = result[:, x * CZ : (x + 1) * CZ]
        places = pl.ds(first_x, count)

        @pl.loop(1, ROWS)
        def _(step):
            target = lax.rem(row + step, ROWS)
            remote(
                send_ref.at[places, target],
                turned_ref.at[row, places],
                send_sems.at[1],
                turned_sem,
                target,
                col,
            ).start()

    turned_ref[row] = send_ref[:, row]
    fetches[2].wait()
    fetches[3].wait()
    influence = jnp.concatenate(
        [influence_ref[pl.ds(j, KX, stride=width), :] for j in range(width)], axis=1
    )
    remote(
        turned_ref.at[0 : ROWS - 1],
        turned_ref.at[0 : ROWS - 1],
        send_sems.at[1],
        turned_sem,
        row_after,
        col,
    ).wait()

    turned_flat = turned_ref.reshape(KX * width, CZ)
    field = jnp.concatenate(
        [turned_flat[pl.ds(j, KX, stride=width), :] for j in range(width)], axis=1
    )
    high, low = split(field)
    spectrum = influence * dot3(table_x_ref[0], table_x_ref[1], high, low)
    high, low = split(spectrum)
    result = dot3(table_x_ref[0], table_x_ref[1], high, low)
    back_flat = back_ref.reshape(KX * width, CZ)
    for j in range(width):
        back_flat[pl.ds(j, KX, stride=width), :] = result[:, j * CZ : (j + 1) * CZ]

    count = CX // GATHER_GROUPS
    for group in range(GATHER_GROUPS):
        places = pl.ds(group * count, count)

        @pl.loop(1, ROWS)
        def _(step):
            target = lax.rem(row + step, ROWS)
            remote(
                back_ref.at[target, places],
                returned_ref.at[places, row],
                send_sems.at[2],
                returned_sems.at[group],
                target,
                col,
            ).start()

    returned_ref[:, row] = back_ref[row]

    returned_flat = returned_ref.reshape(CX, KY, CZ)
    for group in range(GATHER_GROUPS):
        places = slice(group * count, (group + 1) * count)
        remote(
            returned_ref.at[places, 0 : ROWS - 1],
            returned_ref.at[places, 0 : ROWS - 1],
            send_sems.at[2],
            returned_sems.at[group],
            row_after,
            col,
        ).wait_recv()
        field = jnp.concatenate(
            [returned_flat[group * count + x] for x in range(count)], axis=1
        )
        high, low = split(field)
        result = dot3(table_y_ref[0], table_y_ref[1], high, low)
        for x in range(count):
            acc_ref[x] = result[:, x * CZ : (x + 1) * CZ]

        @pl.loop(1, blocks + 1)
        def _(step):
            index = lax.rem(col + step, blocks)
            part = lax.rem(index, COLS)
            plain_y = dense_y_ref[index, 0]
            slope_y = dense_y_ref[index, 1]
            rows = pl.ds(pl.multiple_of(part * CY, CY), PATCH_Y)
            patch = jnp.concatenate([acc_ref[x, rows, :] for x in range(count)], axis=0)
            high, low = split(patch)
            both = jnp.concatenate([high, low], axis=1)

            def contract(place):
                wave_high = z_ref[index, place * CZ : (place + 1) * CZ]
                wave_low = z_ref[index, (place + 1) * CZ : (place + 2) * CZ]
                twice = jnp.concatenate([wave_high, wave_high], axis=0)
                return dot(both, twice) + dot(high, wave_low)

            plain = contract(0)
            third = contract(2)
            if group == 0:
                sums = [0.0] * 4
            else:
                sums = [partial_ref[index, k : k + 1] for k in range(4)]
            for x in range(count):
                here = plain[x * PATCH_Y : (x + 1) * PATCH_Y]
                there = third[x * PATCH_Y : (x + 1) * PATCH_Y]
                inner = jnp.sum(plain_y * here, axis=0, keepdims=True)
                along_y = jnp.sum(slope_y * here, axis=0, keepdims=True)
                along_z = jnp.sum(plain_y * there, axis=0, keepdims=True)
                place = group * count + x
                plain_x = dense_x_ref[index, 0, place : place + 1, :]
                slope_x = dense_x_ref[index, 1, place : place + 1, :]
                sums[0] = sums[0] + plain_x * inner
                sums[1] = sums[1] + slope_x * inner
                sums[2] = sums[2] + plain_x * along_y
                sums[3] = sums[3] + plain_x * along_z
            for k in range(4):
                partial_ref[index, k : k + 1] = sums[k]
            if group == GATHER_GROUPS - 1:
                behind = index // COLS

                @pl.when(step < blocks)
                def _():
                    remote(
                        partial_ref.at[index],
                        arrived_ref.at[behind * COLS + col],
                        send_sems.at[3],
                        arrived_sem,
                        lax.rem(row + ROWS - behind, ROWS),
                        part,
                    ).start()

    arrived_ref[col] = partial_ref[col]
    remote(
        arrived_ref.at[0 : blocks - 1],
        arrived_ref.at[0 : blocks - 1],
        send_sems.at[3],
        arrived_sem,
        row_after,
        col,
    ).wait()
    total = arrived_ref[0]
    for index in range(1, blocks):
        total = total + arrived_ref[index]
    out_charges_ref[...] = jnp.where(live, total[0:1], 0.0)
    out_coords_ref[...] = atoms_ref[col, 7:8, :] * total[1:4]
    remote(
        returned_ref.at[:, 0 : ROWS - 1],
        returned_ref.at[:, 0 : ROWS - 1],
        send_sems.at[2],
        returned_sems.at[0],
        row_after,
        col,
    ).wait_send()


def shape(dims, kind=FLOAT):
    return jax.ShapeDtypeStruct(dims, kind)


def per_device(charges, fractions, base_cells, counts, influence):
    tables = [jnp.asarray(t) for t in make_tables()]
    width = KY // ROWS
    blocks = 2 * COLS
    anywhere = pl.BlockSpec(memory_space=pltpu.HBM)
    vector = pl.BlockSpec(memory_space=pltpu.VMEM)
    dma = pltpu.SemaphoreType.DMA
    grad_charges, grad_coords = pl.pallas_call(
        kernel,
        out_shape=(shape((1, SLOTS)), shape((3, SLOTS))),
        in_specs=[vector, vector, vector, pl.BlockSpec(memory_space=pltpu.SMEM)] + [anywhere] * 4,
        out_specs=(vector, vector),
        scratch_shapes=[
            pltpu.VMEM((KX * width, CZ), FLOAT),
            pltpu.VMEM(tables[0].shape, HIGH_TYPE),
            pltpu.VMEM(tables[1].shape, HIGH_TYPE),
            pltpu.VMEM(tables[2].shape[1:], HIGH_TYPE),
            pltpu.VMEM((blocks, 8, SLOTS), FLOAT),
            pltpu.VMEM((3, 2 * ORDER, blocks, SLOTS), FLOAT),
            pltpu.VMEM((blocks, 3, 8, SLOTS), FLOAT),
            pltpu.VMEM((blocks, 2, PATCH_Y, SLOTS), FLOAT),
            pltpu.VMEM((blocks, 4 * CZ, SLOTS), HIGH_TYPE),
            pltpu.VMEM((CX, KY + 8, CZ), FLOAT),
            pltpu.VMEM((CX, ROWS, width, CZ), FLOAT),
            pltpu.VMEM((ROWS, CX, width, CZ), FLOAT),
            pltpu.VMEM((ROWS, CX, width, CZ), FLOAT),
            pltpu.VMEM((CX, ROWS, width, CZ), FLOAT),
            pltpu.VMEM((blocks, 4, SLOTS), FLOAT),
            pltpu.VMEM((blocks, 4, SLOTS), FLOAT),
            dma((4,)),
            dma((4,)),
            dma,
            dma,
            dma((GATHER_GROUPS,)),
            dma,
        ],
        compiler_params=pltpu.CompilerParams(
            collective_id=0, has_side_effects=True, vmem_limit_bytes=VMEM_LIMIT
        ),
    )(
        charges.reshape(1, SLOTS),
        fractions,
        base_cells,
        counts,
        influence.reshape(KX * width, CZ),
        *tables,
    )
    return grad_charges.reshape(SLOTS), grad_coords


def solution(mesh):
    return jax.shard_map(
        per_device,
        mesh=mesh,
        in_specs=(
            P(("row", "col")),
            P(None, ("row", "col")),
            P(None, ("row", "col")),
            P(("row", "col")),
            P(None, "row", "col"),
        ),
        out_specs=(P(("row", "col")), P(None, ("row", "col"))),
        check_vma=False,
    )
```

```python
import math

import jax
import jax.numpy as jnp
import ml_dtypes
import numpy as np
from jax import lax
from jax.experimental import pallas as pl
from jax.experimental.pallas import tpu as pltpu
from jax.sharding import PartitionSpec as P

KX = 384
KY = 256
KZ = 512
ORDER = 6
SLOTS = 512
ROWS = 64
COLS = 4
CX = KX // ROWS
CY = KY // COLS
CZ = KZ // COLS
PATCH_Y = 72
FINE = 8
COARSE = KZ // FINE
FAN = 2 * FINE
VMEM_LIMIT = 63 * 1024 * 1024
UNROLL = 8
SPREAD_GROUPS = 2
GATHER_GROUPS = 2
MESH = pl.DeviceIdType.MESH

HIGH_TYPE = jnp.bfloat16
FLOAT = jnp.float32


def split_table(table):
    high = table.astype(np.float32).astype(ml_dtypes.bfloat16)
    low = (table - high.astype(np.float64)).astype(np.float32).astype(ml_dtypes.bfloat16)
    return high, low


def cas(product, length):
    angles = (product % length) * (2.0 * math.pi / length)
    return np.cos(angles) + np.sin(angles)


def make_tables():
    kx = np.arange(KX)
    table_x = np.zeros((2, KX + 8, KX), ml_dtypes.bfloat16)
    table_x[:, :KX] = split_table(cas(kx[:, None] * kx[None, :], KX))
    ky = np.arange(KY)
    y = np.arange(KY + 8)
    table_y = np.stack(split_table(cas(y[:, None] * ky[None, :], KY)))
    kz = np.arange(KZ)
    coarse = (kz[:, None] * np.arange(COARSE)[None, :] * FINE % KZ) * (2.0 * math.pi / KZ)
    fine = kz[:, None] * np.arange(FAN)[None, :]
    table_z = np.zeros((COLS, 4 * CZ, 3 * FAN + 2 * COARSE), ml_dtypes.bfloat16)
    for place, values in ((0, np.cos(coarse)), (1, np.sin(coarse))):
        high, low = split_table(values)
        rows = slice(place * CZ, (place + 1) * CZ)
        table_z[:, rows, 3 * FAN : 3 * FAN + COARSE] = high.reshape(COLS, CZ, COARSE)
        table_z[:, rows, 3 * FAN + COARSE :] = low.reshape(COLS, CZ, COARSE)
    for place, values in ((2, cas(fine, KZ)), (3, cas(-fine, KZ))):
        high, low = split_table(values)
        rows = slice(place * CZ, (place + 1) * CZ)
        table_z[:, rows, :FAN] = high.reshape(COLS, CZ, FAN)
        table_z[:, rows, FAN : 2 * FAN] = high.reshape(COLS, CZ, FAN)
        table_z[:, rows, 2 * FAN : 3 * FAN] = low.reshape(COLS, CZ, FAN)
    return table_x, table_y, np.pad(table_z, ((0, 0), (0, 8), (0, 0)))


def spline_tables(fraction):
    previous = [fraction, 1.0 - fraction]
    fifth_order = previous
    for degree in range(3, 7):
        current = []
        for position in range(degree):
            summed = None
            if position < degree - 1:
                summed = (fraction + position) * previous[position]
            if position >= 1:
                second = (degree - fraction - position) * previous[position - 1]
                summed = second if summed is None else summed + second
            current.append(summed * (1.0 / (degree - 1)))
        fifth_order = previous
        previous = current
    slopes = []
    for position in range(6):
        if position == 0:
            slopes.append(fifth_order[0])
        elif position == 5:
            slopes.append(-fifth_order[4])
        else:
            slopes.append(fifth_order[position] - fifth_order[position - 1])
    return previous[::-1], slopes[::-1]


def split(value):
    high = value.astype(HIGH_TYPE)
    return high, (value - high.astype(FLOAT)).astype(HIGH_TYPE)


def dot(left, right, transposed=False):
    dims = (((1,), (1 if transposed else 0,)), ((), ()))
    return lax.dot_general(left, right, dims, preferred_element_type=FLOAT)


def dot3(left_high, left_low, right_high, right_low):
    return (
        dot(left_high, right_high) + dot(left_high, right_low) + dot(left_low, right_high)
    )


def dense(base, weights, rows):
    distance = lax.broadcasted_iota(jnp.int32, (rows, SLOTS), 0).astype(FLOAT) - base
    total = jnp.zeros((rows, SLOTS), FLOAT)
    for offset in range(ORDER):
        total = jnp.where(distance == offset, weights[offset], total)
    return total


def kernel(
    charges_ref,
    fractions_ref,
    cells_ref,
    counts_ref,
    influence_hbm,
    table_x_hbm,
    table_y_hbm,
    table_z_hbm,
    out_charges_ref,
    out_coords_ref,
    influence_ref,
    table_x_ref,
    table_y_ref,
    table_z_ref,
    atoms_ref,
    spline_ref,
    dense_x_ref,
    dense_y_ref,
    z_ref,
    turn_ref,
    acc_ref,
    send_ref,
    turned_ref,
    back_ref,
    returned_ref,
    partial_ref,
    arrived_ref,
    local_sems,
    send_sems,
    atoms_sem,
    turned_sem,
    returned_sems,
    arrived_sem,
):
    row = lax.axis_index("row")
    col = lax.axis_index("col")
    row_after = lax.rem(row + 1, ROWS)
    row_before = lax.rem(row + ROWS - 1, ROWS)
    width = KY // ROWS
    blocks = 2 * COLS

    barrier = pltpu.get_barrier_semaphore()

    def greet(device_row, device_col):
        pl.semaphore_signal(
            barrier, inc=1, device_id=(device_row, device_col), device_id_type=MESH
        )

    for step in range(1, COLS):
        other = lax.rem(col + step, COLS)
        greet(row, other)
        greet(row_after, other)
        greet(row_before, other)

    @pl.loop(1, ROWS)
    def _(step):
        greet(lax.rem(row + step, ROWS), col)

    fetches = [
        pltpu.make_async_copy(table_z_hbm.at[col], table_z_ref, local_sems.at[0]),
        pltpu.make_async_copy(table_y_hbm, table_y_ref, local_sems.at[1]),
        pltpu.make_async_copy(table_x_hbm, table_x_ref, local_sems.at[2]),
        pltpu.make_async_copy(influence_hbm, influence_ref, local_sems.at[3]),
    ]
    for fetch in fetches:
        fetch.start()

    slot = lax.broadcasted_iota(jnp.int32, (1, SLOTS), 1)
    live = slot < counts_ref[0]
    weight = jnp.where(live, charges_ref[...], 0.0)
    atoms_ref[col, 0:1, :] = weight
    atoms_ref[col, 1:4, :] = fractions_ref[...]
    cells = cells_ref[...]
    atoms_ref[col, 4:5, :] = (cells[0:1] - row * CX).astype(FLOAT)
    atoms_ref[col, 5:6, :] = (cells[1:2] - col * CY).astype(FLOAT)
    atoms_ref[col, 6:7, :] = cells[2:3].astype(FLOAT)
    atoms_ref[col, 7:8, :] = weight

    pl.semaphore_wait(barrier, ROWS - 1 + 3 * (COLS - 1))

    def remote(source, target, send_sem, recv_sem, device_row, device_col):
        return pltpu.make_async_remote_copy(
            src_ref=source,
            dst_ref=target,
            send_sem=send_sem,
            recv_sem=recv_sem,
            device_id=(device_row, device_col),
            device_id_type=MESH,
        )

    for step in range(1, COLS):
        other = lax.rem(col + step, COLS)
        remote(
            atoms_ref.at[col], atoms_ref.at[col], send_sems.at[0], atoms_sem, row, other
        ).start()
    for step in range(COLS):
        other = lax.rem(col + step, COLS)
        remote(
            atoms_ref.at[col],
            atoms_ref.at[COLS + col],
            send_sems.at[0],
            atoms_sem,
            row_after,
            other,
        ).start()
    remote(
        atoms_ref.at[0 : blocks - 1],
        atoms_ref.at[0 : blocks - 1],
        send_sems.at[0],
        atoms_sem,
        row_after,
        col,
    ).wait()

    for dim in range(3):
        values, slopes = spline_tables(atoms_ref[:, 1 + dim, :])
        for offset in range(ORDER):
            spline_ref[dim, offset] = values[offset]
            spline_ref[dim, ORDER + offset] = slopes[offset]
    fetches[0].wait()

    @pl.loop(0, blocks, unroll=UNROLL)
    def _(index):
        shift = (CX * (index // COLS)).astype(FLOAT)
        weight = atoms_ref[index, 0:1, :]
        base_x = atoms_ref[index, 4:5, :] - shift
        base_y = atoms_ref[index, 5:6, :]
        base_z = atoms_ref[index, 6:7, :]

        def rows(dim, place):
            return [
                spline_ref[dim, place + offset, pl.ds(index, 1), :] for offset in range(ORDER)
            ]

        dense_x_ref[index, 2] = weight * dense(base_x, rows(0, 0), 8)
        dense_y_ref[index, 0] = dense(base_y, rows(1, 0), PATCH_Y)
        coarse = jnp.floor(base_z * (1.0 / FINE))
        rest = base_z - coarse * FINE
        hit = lax.broadcasted_iota(jnp.int32, (COARSE, SLOTS), 0).astype(FLOAT) == coarse
        hit = jnp.where(hit, 1.0, 0.0).astype(HIGH_TYPE)
        fine_high, fine_low = split(dense(rest, rows(2, 0), FAN))
        joined = jnp.concatenate([fine_high, fine_low, fine_high, hit, hit], axis=0)
        parts = dot(table_z_ref[: 4 * CZ], joined)
        cosine, sine = parts[:CZ], parts[CZ : 2 * CZ]
        turn_ref[index, :CZ] = cosine
        turn_ref[index, CZ:] = sine
        wave = cosine * parts[2 * CZ : 3 * CZ] + sine * parts[3 * CZ :]
        wave_high, wave_low = split(wave)
        z_ref[index, 0:CZ] = wave_high
        z_ref[index, CZ : 2 * CZ] = wave_low

    send_flat = send_ref.reshape(CX, KY, CZ)
    for group in range(SPREAD_GROUPS):
        count = CX // SPREAD_GROUPS
        first_x = group * count
        acc_ref[0:count] = jnp.zeros((count, KY + 8, CZ), FLOAT)

        @pl.loop(0, blocks, unroll=UNROLL)
        def _(index):
            part = lax.rem(index, COLS)
            plain_y = dense_y_ref[index, 0]
            patch = jnp.concatenate(
                [dense_x_ref[index, 2, x : x + 1, :] * plain_y for x in range(first_x, first_x + count)],
                axis=0,
            )
            high, low = split(patch)
            both = dot(high, z_ref[index, 0 : 2 * CZ], True)
            summed = both[:, :CZ] + both[:, CZ:] + dot(low, z_ref[index, 0:CZ], True)
            rows = pl.ds(pl.multiple_of(part * CY, CY), PATCH_Y)
            for x in range(count):
                acc_ref[x, rows, :] += summed[x * PATCH_Y : (x + 1) * PATCH_Y]

        if group == 0:
            fetches[1].wait()
        for x in range(count):
            acc_ref[x, 0:8, :] += acc_ref[x, KY : KY + 8, :]
        field = jnp.concatenate([acc_ref[x, :KY] for x in range(count)], axis=1)
        high, low = split(field)
        result = dot3(table_y_ref[0, :KY], table_y_ref[1, :KY], high, low)
        for x in range(count):
            send_flat[first_x + x] = result[:, x * CZ : (x + 1) * CZ]
        places = pl.ds(first_x, count)

        @pl.loop(1, ROWS)
        def _(step):
            target = lax.rem(row + step, ROWS)
            remote(
                send_ref.at[places, target],
                turned_ref.at[row, places],
                send_sems.at[1],
                turned_sem,
                target,
                col,
            ).start()

    @pl.loop(0, blocks, unroll=UNROLL)
    def _(index):
        base_x = atoms_ref[index, 4:5, :] - (CX * (index // COLS)).astype(FLOAT)
        base_y = atoms_ref[index, 5:6, :]
        base_z = atoms_ref[index, 6:7, :]

        def rows(dim, place):
            return [
                spline_ref[dim, place + offset, pl.ds(index, 1), :] for offset in range(ORDER)
            ]

        dense_x_ref[index, 0] = dense(base_x, rows(0, 0), 8)
        dense_x_ref[index, 1] = dense(base_x, rows(0, ORDER), 8)
        dense_y_ref[index, 1] = dense(base_y, rows(1, ORDER), PATCH_Y)
        rest = base_z - jnp.floor(base_z * (1.0 / FINE)) * FINE
        high, low = split(dense(rest, rows(2, ORDER), FAN))
        joined = jnp.concatenate([high, low, high], axis=0)
        parts = dot(table_z_ref[2 * CZ : 4 * CZ, : 3 * FAN], joined)
        wave = turn_ref[index, :CZ] * parts[:CZ] + turn_ref[index, CZ:] * parts[CZ:]
        high, low = split(wave)
        z_ref[index, 2 * CZ : 3 * CZ] = high
        z_ref[index, 3 * CZ :] = low

    turned_ref[row] = send_ref[:, row]
    fetches[2].wait()
    fetches[3].wait()
    influence = jnp.concatenate(
        [influence_ref[pl.ds(j, KX, stride=width), :] for j in range(width)], axis=1
    )
    remote(
        turned_ref.at[0 : ROWS - 1],
        turned_ref.at[0 : ROWS - 1],
        send_sems.at[1],
        turned_sem,
        row_after,
        col,
    ).wait()

    turned_flat = turned_ref.reshape(KX * width, CZ)
    field = jnp.concatenate(
        [turned_flat[pl.ds(j, KX, stride=width), :] for j in range(width)], axis=1
    )
    high, low = split(field)
    spectrum = influence * dot3(table_x_ref[0, :KX], table_x_ref[1, :KX], high, low)
    high, low = split(spectrum)
    result = dot3(table_x_ref[0, :KX], table_x_ref[1, :KX], high, low)
    back_flat = back_ref.reshape(KX * width, CZ)
    for j in range(width):
        back_flat[pl.ds(j, KX, stride=width), :] = result[:, j * CZ : (j + 1) * CZ]

    count = CX // GATHER_GROUPS
    for group in range(GATHER_GROUPS):
        places = pl.ds(group * count, count)

        @pl.loop(1, ROWS)
        def _(step):
            target = lax.rem(row + step, ROWS)
            remote(
                back_ref.at[target, places],
                returned_ref.at[places, row],
                send_sems.at[2],
                returned_sems.at[group],
                target,
                col,
            ).start()

    returned_ref[:, row] = back_ref[row]

    returned_flat = returned_ref.reshape(CX, KY, CZ)
    for group in range(GATHER_GROUPS):
        places = slice(group * count, (group + 1) * count)
        remote(
            returned_ref.at[places, 0 : ROWS - 1],
            returned_ref.at[places, 0 : ROWS - 1],
            send_sems.at[2],
            returned_sems.at[group],
            row_after,
            col,
        ).wait_recv()
        field = jnp.concatenate(
            [returned_flat[group * count + x] for x in range(count)], axis=1
        )
        high, low = split(field)
        result = dot3(table_y_ref[0], table_y_ref[1], high, low)
        for x in range(count):
            acc_ref[x] = result[:, x * CZ : (x + 1) * CZ]

        @pl.loop(1, blocks + 1, unroll=UNROLL)
        def _(step):
            index = lax.rem(col + step, blocks)
            part = lax.rem(index, COLS)
            plain_y = dense_y_ref[index, 0]
            slope_y = dense_y_ref[index, 1]
            rows = pl.ds(pl.multiple_of(part * CY, CY), PATCH_Y)
            patch = jnp.concatenate([acc_ref[x, rows, :] for x in range(count)], axis=0)
            high, low = split(patch)
            both = jnp.concatenate([high, low], axis=1)

            def contract(place):
                wave_high = z_ref[index, place * CZ : (place + 1) * CZ]
                wave_low = z_ref[index, (place + 1) * CZ : (place + 2) * CZ]
                twice = jnp.concatenate([wave_high, wave_high], axis=0)
                return dot(both, twice) + dot(high, wave_low)

            plain = contract(0)
            third = contract(2)
            if group == 0:
                sums = [0.0] * 4
            else:
                sums = [partial_ref[index, k : k + 1] for k in range(4)]
            for x in range(count):
                here = plain[x * PATCH_Y : (x + 1) * PATCH_Y]
                there = third[x * PATCH_Y : (x + 1) * PATCH_Y]
                inner = jnp.sum(plain_y * here, axis=0, keepdims=True)
                along_y = jnp.sum(slope_y * here, axis=0, keepdims=True)
                along_z = jnp.sum(plain_y * there, axis=0, keepdims=True)
                place = group * count + x
                plain_x = dense_x_ref[index, 0, place : place + 1, :]
                slope_x = dense_x_ref[index, 1, place : place + 1, :]
                sums[0] = sums[0] + plain_x * inner
                sums[1] = sums[1] + slope_x * inner
                sums[2] = sums[2] + plain_x * along_y
                sums[3] = sums[3] + plain_x * along_z
            for k in range(4):
                partial_ref[index, k : k + 1] = sums[k]
            if group == GATHER_GROUPS - 1:
                behind = index // COLS

                @pl.when(step < blocks)
                def _():
                    remote(
                        partial_ref.at[index],
                        arrived_ref.at[behind * COLS + col],
                        send_sems.at[3],
                        arrived_sem,
                        lax.rem(row + ROWS - behind, ROWS),
                        part,
                    ).start()

    arrived_ref[col] = partial_ref[col]
    remote(
        arrived_ref.at[0 : blocks - 1],
        arrived_ref.at[0 : blocks - 1],
        send_sems.at[3],
        arrived_sem,
        row_after,
        col,
    ).wait()
    total = arrived_ref[0]
    for index in range(1, blocks):
        total = total + arrived_ref[index]
    out_charges_ref[...] = jnp.where(live, total[0:1], 0.0)
    out_coords_ref[...] = atoms_ref[col, 7:8, :] * total[1:4]
    remote(
        returned_ref.at[:, 0 : ROWS - 1],
        returned_ref.at[:, 0 : ROWS - 1],
        send_sems.at[2],
        returned_sems.at[0],
        row_after,
        col,
    ).wait_send()


def shape(dims, kind=FLOAT):
    return jax.ShapeDtypeStruct(dims, kind)


def per_device(charges, fractions, base_cells, counts, influence):
    tables = [jnp.asarray(t) for t in make_tables()]
    width = KY // ROWS
    blocks = 2 * COLS
    anywhere = pl.BlockSpec(memory_space=pltpu.HBM)
    vector = pl.BlockSpec(memory_space=pltpu.VMEM)
    dma = pltpu.SemaphoreType.DMA
    grad_charges, grad_coords = pl.pallas_call(
        kernel,
        out_shape=(shape((1, SLOTS)), shape((3, SLOTS))),
        in_specs=[vector, vector, vector, pl.BlockSpec(memory_space=pltpu.SMEM)] + [anywhere] * 4,
        out_specs=(vector, vector),
        scratch_shapes=[
            pltpu.VMEM((KX * width, CZ), FLOAT),
            pltpu.VMEM(tables[0].shape, HIGH_TYPE),
            pltpu.VMEM(tables[1].shape, HIGH_TYPE),
            pltpu.VMEM(tables[2].shape[1:], HIGH_TYPE),
            pltpu.VMEM((blocks, 8, SLOTS), FLOAT),
            pltpu.VMEM((3, 2 * ORDER, blocks, SLOTS), FLOAT),
            pltpu.VMEM((blocks, 3, 8, SLOTS), FLOAT),
            pltpu.VMEM((blocks, 2, PATCH_Y, SLOTS), FLOAT),
            pltpu.VMEM((blocks, 4 * CZ, SLOTS), HIGH_TYPE),
            pltpu.VMEM((blocks, 2 * CZ, SLOTS), FLOAT),
            pltpu.VMEM((CX, KY + 8, CZ), FLOAT),
            pltpu.VMEM((CX, ROWS, width, CZ), FLOAT),
            pltpu.VMEM((ROWS, CX, width, CZ), FLOAT),
            pltpu.VMEM((ROWS, CX, width, CZ), FLOAT),
            pltpu.VMEM((CX, ROWS, width, CZ), FLOAT),
            pltpu.VMEM((blocks, 4, SLOTS), FLOAT),
            pltpu.VMEM((blocks, 4, SLOTS), FLOAT),
            dma((4,)),
            dma((4,)),
            dma,
            dma,
            dma((GATHER_GROUPS,)),
            dma,
        ],
        compiler_params=pltpu.CompilerParams(
            collective_id=0, has_side_effects=True, vmem_limit_bytes=VMEM_LIMIT
        ),
    )(
        charges.reshape(1, SLOTS),
        fractions,
        base_cells,
        counts,
        influence.reshape(KX * width, CZ),
        *tables,
    )
    return grad_charges.reshape(SLOTS), grad_coords


def solution(mesh):
    return jax.shard_map(
        per_device,
        mesh=mesh,
        in_specs=(
            P(("row", "col")),
            P(None, ("row", "col")),
            P(None, ("row", "col")),
            P(("row", "col")),
            P(None, "row", "col"),
        ),
        out_specs=(P(("row", "col")), P(None, ("row", "col"))),
        check_vma=False,
    )
```

```python
import math

import jax
import jax.numpy as jnp
import ml_dtypes
import numpy as np
from jax import lax
from jax.experimental import pallas as pl
from jax.experimental.pallas import tpu as pltpu
from jax.sharding import PartitionSpec as P

KX = 384
KY = 256
KZ = 512
ORDER = 6
SLOTS = 512
ROWS = 64
COLS = 4
CX = KX // ROWS
CY = KY // COLS
CZ = KZ // COLS
PATCH_Y = 72
FINE = 8
COARSE = KZ // FINE
FAN = 2 * FINE
VMEM_LIMIT = 63 * 1024 * 1024
GATHER_GROUPS = 1
HALVES = 2
WIDTH = KY // ROWS
PART = WIDTH // HALVES
BLOCKS = 2 * COLS
MESH = pl.DeviceIdType.MESH

HIGH_TYPE = jnp.bfloat16
FLOAT = jnp.float32


def split_table(table):
    high = table.astype(np.float32).astype(ml_dtypes.bfloat16)
    low = (table - high.astype(np.float64)).astype(np.float32).astype(ml_dtypes.bfloat16)
    return high, low


def cas(product, length):
    angles = (product % length) * (2.0 * math.pi / length)
    return np.cos(angles) + np.sin(angles)


def make_tables():
    kx = np.arange(KX)
    table_x = np.zeros((2, KX + 8, KX), ml_dtypes.bfloat16)
    table_x[:, :KX] = split_table(cas(kx[:, None] * kx[None, :], KX))
    ky = np.arange(KY).reshape(ROWS, HALVES, PART).transpose(1, 0, 2).reshape(KY)
    y = np.arange(KY + 8)
    table_y = np.stack(split_table(cas(ky[:, None] * np.arange(KY)[None, :], KY)))
    table_y = np.pad(table_y, ((0, 0), (0, 8), (0, 0)))
    table_back = np.stack(split_table(cas(y[:, None] * ky[None, :], KY)))
    kz = np.arange(KZ)
    coarse = (kz[:, None] * np.arange(COARSE)[None, :] * FINE % KZ) * (2.0 * math.pi / KZ)
    fine = kz[:, None] * np.arange(FAN)[None, :]
    table_z = np.zeros((COLS, 4 * CZ, 3 * FAN + 2 * COARSE), ml_dtypes.bfloat16)
    for place, values in ((0, np.cos(coarse)), (1, np.sin(coarse))):
        high, low = split_table(values)
        rows = slice(place * CZ, (place + 1) * CZ)
        table_z[:, rows, 3 * FAN : 3 * FAN + COARSE] = high.reshape(COLS, CZ, COARSE)
        table_z[:, rows, 3 * FAN + COARSE :] = low.reshape(COLS, CZ, COARSE)
    for place, values in ((2, cas(fine, KZ)), (3, cas(-fine, KZ))):
        high, low = split_table(values)
        rows = slice(place * CZ, (place + 1) * CZ)
        table_z[:, rows, :FAN] = high.reshape(COLS, CZ, FAN)
        table_z[:, rows, FAN : 2 * FAN] = high.reshape(COLS, CZ, FAN)
        table_z[:, rows, 2 * FAN : 3 * FAN] = low.reshape(COLS, CZ, FAN)
    return table_x, table_y, table_back, np.pad(table_z, ((0, 0), (0, 8), (0, 0)))


def spline_tables(fraction):
    previous = [fraction, 1.0 - fraction]
    fifth_order = previous
    for degree in range(3, 7):
        current = []
        for position in range(degree):
            summed = None
            if position < degree - 1:
                summed = (fraction + position) * previous[position]
            if position >= 1:
                second = (degree - fraction - position) * previous[position - 1]
                summed = second if summed is None else summed + second
            current.append(summed * (1.0 / (degree - 1)))
        fifth_order = previous
        previous = current
    slopes = []
    for position in range(6):
        if position == 0:
            slopes.append(fifth_order[0])
        elif position == 5:
            slopes.append(-fifth_order[4])
        else:
            slopes.append(fifth_order[position] - fifth_order[position - 1])
    return previous[::-1], slopes[::-1]


def split(value):
    high = value.astype(HIGH_TYPE)
    return high, (value - high.astype(FLOAT)).astype(HIGH_TYPE)


def dot(left, right, transposed=False):
    dims = (((1,), (1 if transposed else 0,)), ((), ()))
    return lax.dot_general(left, right, dims, preferred_element_type=FLOAT)


def dot3(left_high, left_low, right_high, right_low):
    return (
        dot(left_high, right_high) + dot(left_high, right_low) + dot(left_low, right_high)
    )


def dense(base, weights, rows):
    distance = lax.broadcasted_iota(jnp.int32, (rows, SLOTS), 0).astype(FLOAT) - base
    total = jnp.zeros((rows, SLOTS), FLOAT)
    for offset in range(ORDER):
        total = jnp.where(distance == offset, weights[offset], total)
    return total


def kernel(
    charges_ref,
    fractions_ref,
    cells_ref,
    counts_ref,
    influence_hbm,
    table_x_hbm,
    table_y_hbm,
    table_back_hbm,
    table_z_hbm,
    out_ref,
    influence_ref,
    table_x_ref,
    table_y_ref,
    table_back_ref,
    table_z_ref,
    atoms_ref,
    slope_ref,
    dense_x_ref,
    dense_y_ref,
    z_ref,
    turn_ref,
    acc_ref,
    send_ref,
    turned_ref,
    back_ref,
    returned_ref,
    partial_ref,
    arrived_ref,
    local_sems,
    send_sems,
    atoms_sems,
    turned_sems,
    returned_sems,
    arrived_sem,
):
    row = lax.axis_index("row")
    col = lax.axis_index("col")
    half_at = col // 2
    core = lax.rem(col, 2)
    row_after = lax.rem(row + 1, ROWS)
    row_before = lax.rem(row + ROWS - 1, ROWS)
    sibling = half_at * 2 + 1 - core
    far_cols = [(1 - half_at) * 2 + core, (1 - half_at) * 2 + 1 - core]

    barrier = pltpu.get_barrier_semaphore()

    def greet(device_row, device_col):
        pl.semaphore_signal(
            barrier, inc=1, device_id=(device_row, device_col), device_id_type=MESH
        )

    for other in far_cols + [sibling]:
        greet(row, other)
        greet(row_after, other)
        greet(row_before, other)

    @pl.loop(1, ROWS)
    def _(step):
        greet(lax.rem(row + step, ROWS), col)

    fetches = [
        pltpu.make_async_copy(table_z_hbm.at[col], table_z_ref, local_sems.at[0]),
        pltpu.make_async_copy(table_y_hbm, table_y_ref, local_sems.at[1]),
        pltpu.make_async_copy(table_x_hbm, table_x_ref, local_sems.at[2]),
        pltpu.make_async_copy(influence_hbm, influence_ref, local_sems.at[3]),
        pltpu.make_async_copy(table_back_hbm, table_back_ref, local_sems.at[4]),
    ]
    for fetch in fetches:
        fetch.start()

    slot = lax.broadcasted_iota(jnp.int32, (1, SLOTS), 1)
    weight = jnp.where(slot < counts_ref[0], charges_ref[...], 0.0)
    atoms_ref[col, 0:1, :] = weight
    atoms_ref[col, 1:4, :] = fractions_ref[...]
    cells = cells_ref[...]
    atoms_ref[col, 4:5, :] = (cells[0:1] - row * CX).astype(FLOAT)
    atoms_ref[col, 5:6, :] = (cells[1:2] - col * CY).astype(FLOAT)
    atoms_ref[col, 6:7, :] = cells[2:3].astype(FLOAT)
    atoms_ref[col, 7:8, :] = weight
    acc_ref[...] = jnp.zeros(acc_ref.shape, FLOAT)

    def remote(source, target, send_sem, recv_sem, device_row, device_col):
        return pltpu.make_async_remote_copy(
            src_ref=source,
            dst_ref=target,
            send_sem=send_sem,
            recv_sem=recv_sem,
            device_id=(device_row, device_col),
            device_id_type=MESH,
        )

    def bases(index, behind):
        base_x = atoms_ref[index, 4:5, :] + float(CX) * (-behind)
        base_z = atoms_ref[index, 6:7, :]
        coarse = jnp.floor(base_z * (1.0 / FINE))
        return base_x, atoms_ref[index, 5:6, :], coarse, base_z - coarse * FINE

    def prepare(index, behind):
        values, slopes = spline_tables(atoms_ref[index, 1:4, :])
        for offset in range(ORDER):
            slope_ref[index, offset, 0:3, :] = slopes[offset]
        base_x, base_y, coarse, rest = bases(index, behind)

        def rows(dim):
            return [value[dim : dim + 1] for value in values]

        plain_x = dense(base_x, rows(0), 8)
        dense_x_ref[index, 0] = plain_x
        dense_x_ref[index, 2] = atoms_ref[index, 0:1, :] * plain_x
        dense_y_ref[index, 0] = dense(base_y, rows(1), PATCH_Y)
        hit = lax.broadcasted_iota(jnp.int32, (COARSE, SLOTS), 0).astype(FLOAT) == coarse
        hit = jnp.where(hit, 1.0, 0.0).astype(HIGH_TYPE)
        fine_high, fine_low = split(dense(rest, rows(2), FAN))
        joined = jnp.concatenate([fine_high, fine_low, fine_high, hit, hit], axis=0)
        parts = dot(table_z_ref[: 4 * CZ], joined)
        cosine, sine = parts[:CZ], parts[CZ : 2 * CZ]
        turn_ref[index, :CZ] = cosine
        turn_ref[index, CZ:] = sine
        wave = cosine * parts[2 * CZ : 3 * CZ] + sine * parts[3 * CZ :]
        wave_high, wave_low = split(wave)
        z_ref[index, 0:CZ] = wave_high
        z_ref[index, CZ : 2 * CZ] = wave_low

    def prepare_slopes(index, behind):
        base_x, base_y, coarse, rest = bases(index, behind)

        def rows(dim):
            return [slope_ref[index, offset, dim : dim + 1, :] for offset in range(ORDER)]

        dense_x_ref[index, 1] = dense(base_x, rows(0), 8)
        dense_y_ref[index, 1] = dense(base_y, rows(1), PATCH_Y)
        high, low = split(dense(rest, rows(2), FAN))
        joined = jnp.concatenate([high, low, high], axis=0)
        parts = dot(table_z_ref[2 * CZ : 4 * CZ, : 3 * FAN], joined)
        wave = turn_ref[index, :CZ] * parts[:CZ] + turn_ref[index, CZ:] * parts[CZ:]
        high, low = split(wave)
        z_ref[index, 2 * CZ : 3 * CZ] = high
        z_ref[index, 3 * CZ :] = low

    def spread(index, part):
        plain_y = dense_y_ref[index, 0]
        patch = jnp.concatenate(
            [dense_x_ref[index, 2, x : x + 1, :] * plain_y for x in range(CX)], axis=0
        )
        high, low = split(patch)
        both = dot(high, z_ref[index, 0 : 2 * CZ], True)
        summed = both[:, :CZ] + both[:, CZ:] + dot(low, z_ref[index, 0:CZ], True)
        rows = pl.ds(pl.multiple_of(part * CY, CY), PATCH_Y)
        for x in range(CX):
            acc_ref[x, rows, :] += summed[x * PATCH_Y : (x + 1) * PATCH_Y]

    near = [(0, sibling), (1, col), (1, sibling)]
    far = [(behind, other) for other in far_cols for behind in range(2)]
    fetches[0].wait()
    prepare(col, 0)
    pl.semaphore_wait(barrier, ROWS - 1 + 3 * (COLS - 1))

    for group, members in enumerate((far, near)):
        for behind, other in members:
            remote(
                atoms_ref.at[col],
                atoms_ref.at[behind * COLS + col],
                send_sems.at[0],
                atoms_sems.at[group],
                row_after if behind else row,
                other,
            ).start()
    spread(col, col)
    for group, members in ((1, near), (0, far)):
        count = len(members)
        remote(
            atoms_ref.at[0:count],
            atoms_ref.at[0:count],
            send_sems.at[0],
            atoms_sems.at[group],
            row_after,
            col,
        ).wait_recv()
        for behind, other in members:
            prepare(behind * COLS + other, behind)
        for behind, other in members:
            spread(behind * COLS + other, other)

    fetches[1].wait()
    for x in range(CX):
        acc_ref[x, 0:8, :] += acc_ref[x, KY : KY + 8, :]
    send_flat = send_ref.reshape(HALVES, CX, KY // HALVES, CZ)
    field = jnp.concatenate([acc_ref[x, :KY] for x in range(CX)], axis=1)
    high, low = split(field)
    for half in range(HALVES):
        rows = slice(half * KY // HALVES, (half + 1) * KY // HALVES)
        result = dot3(table_y_ref[0, rows], table_y_ref[1, rows], high, low)
        for x in range(CX):
            send_flat[half, x] = result[:, x * CZ : (x + 1) * CZ]

        @pl.loop(1, ROWS)
        def _(step):
            target = lax.rem(row + step, ROWS)
            remote(
                send_ref.at[half, :, target],
                turned_ref.at[half, row],
                send_sems.at[1],
                turned_sems.at[half],
                target,
                col,
            ).start()

        turned_ref[half, row] = send_ref[half, :, row]

    for behind in range(2):
        for part in far_cols + [col, sibling]:
            prepare_slopes(behind * COLS + part, behind)
    fetches[2].wait()
    fetches[3].wait()
    count = CX // GATHER_GROUPS
    back_flat = back_ref.reshape(HALVES, KX * PART, CZ)
    turned_flat = turned_ref.reshape(HALVES, KX * PART, CZ)
    for half in range(HALVES):
        influence = jnp.concatenate(
            [
                influence_ref[pl.ds(half * PART + j, KX, stride=WIDTH), :]
                for j in range(PART)
            ],
            axis=1,
        )
        remote(
            turned_ref.at[half, 0 : ROWS - 1],
            turned_ref.at[half, 0 : ROWS - 1],
            send_sems.at[1],
            turned_sems.at[half],
            row_after,
            col,
        ).wait_recv()
        field = jnp.concatenate(
            [turned_flat[half, pl.ds(j, KX, stride=PART), :] for j in range(PART)], axis=1
        )
        high, low = split(field)
        spectrum = influence * dot3(table_x_ref[0, :KX], table_x_ref[1, :KX], high, low)
        high, low = split(spectrum)
        result = dot3(table_x_ref[0, :KX], table_x_ref[1, :KX], high, low)
        for j in range(PART):
            back_flat[half, pl.ds(j, KX, stride=PART), :] = result[:, j * CZ : (j + 1) * CZ]
        pieces = 1 if half < HALVES - 1 else GATHER_GROUPS
        for piece in range(pieces):
            planes = pl.ds(piece * (CX // pieces), CX // pieces)

            @pl.loop(1, ROWS)
            def _(step):
                target = lax.rem(row + step, ROWS)
                remote(
                    back_ref.at[half, target, planes],
                    returned_ref.at[half, planes, row],
                    send_sems.at[2],
                    returned_sems.at[half + piece],
                    target,
                    col,
                ).start()

        returned_ref[half, :, row] = back_ref[half, row]

    def returned(half, planes, place):
        return remote(
            returned_ref.at[half, planes, 0 : ROWS - 1],
            returned_ref.at[half, planes, 0 : ROWS - 1],
            send_sems.at[2],
            returned_sems.at[place],
            row_after,
            col,
        )

    fetches[4].wait()
    for half in range(HALVES - 1):
        returned(half, slice(0, CX), half).wait_recv()
    returned_flat = returned_ref.reshape(HALVES, CX, KY // HALVES, CZ)
    order = far + [(1, sibling), (0, sibling), (1, col), (0, col)]
    for group in range(GATHER_GROUPS):
        planes = slice(group * count, (group + 1) * count)
        returned(HALVES - 1, planes, HALVES - 1 + group).wait_recv()
        field = jnp.concatenate(
            [
                jnp.concatenate(
                    [returned_flat[half, group * count + x] for half in range(HALVES)], axis=0
                )
                for x in range(count)
            ],
            axis=1,
        )
        high, low = split(field)
        result = dot3(table_back_ref[0], table_back_ref[1], high, low)
        for x in range(count):
            acc_ref[x] = result[:, x * CZ : (x + 1) * CZ]
        for behind, part in order:
            index = behind * COLS + part
            plain_y = dense_y_ref[index, 0]
            slope_y = dense_y_ref[index, 1]
            rows = pl.ds(pl.multiple_of(part * CY, CY), PATCH_Y)
            patch = jnp.concatenate([acc_ref[x, rows, :] for x in range(count)], axis=0)
            high, low = split(patch)
            both = jnp.concatenate([high, low], axis=1)

            def contract(place):
                wave_high = z_ref[index, place * CZ : (place + 1) * CZ]
                wave_low = z_ref[index, (place + 1) * CZ : (place + 2) * CZ]
                twice = jnp.concatenate([wave_high, wave_high], axis=0)
                return dot(both, twice) + dot(high, wave_low)

            plain = contract(0)
            third = contract(2)
            if group == 0:
                sums = [0.0] * 4
            else:
                sums = [partial_ref[index, k : k + 1] for k in range(4)]
            for x in range(count):
                here = plain[x * PATCH_Y : (x + 1) * PATCH_Y]
                there = third[x * PATCH_Y : (x + 1) * PATCH_Y]
                inner = jnp.sum(plain_y * here, axis=0, keepdims=True)
                along_y = jnp.sum(slope_y * here, axis=0, keepdims=True)
                along_z = jnp.sum(plain_y * there, axis=0, keepdims=True)
                place = group * count + x
                plain_x = dense_x_ref[index, 0, place : place + 1, :]
                slope_x = dense_x_ref[index, 1, place : place + 1, :]
                sums[0] = sums[0] + plain_x * inner
                sums[1] = sums[1] + slope_x * inner
                sums[2] = sums[2] + plain_x * along_y
                sums[3] = sums[3] + plain_x * along_z
            for k in range(4):
                partial_ref[index, k : k + 1] = sums[k]
            if group == GATHER_GROUPS - 1 and not (behind == 0 and part is col):
                remote(
                    partial_ref.at[index],
                    arrived_ref.at[behind * COLS + col],
                    send_sems.at[3],
                    arrived_sem,
                    row_before if behind else row,
                    part,
                ).start()

    arrived_ref[col] = partial_ref[col]
    remote(
        arrived_ref.at[0 : BLOCKS - 1],
        arrived_ref.at[0 : BLOCKS - 1],
        send_sems.at[3],
        arrived_sem,
        row_after,
        col,
    ).wait()
    total = arrived_ref[0]
    for index in range(1, BLOCKS):
        total = total + arrived_ref[index]
    out_ref[...] = total
    remote(
        atoms_ref.at[0 : BLOCKS - 1],
        atoms_ref.at[0 : BLOCKS - 1],
        send_sems.at[0],
        atoms_sems.at[0],
        row_after,
        col,
    ).wait_send()
    remote(
        turned_ref.at[:, 0 : ROWS - 1],
        turned_ref.at[:, 0 : ROWS - 1],
        send_sems.at[1],
        turned_sems.at[0],
        row_after,
        col,
    ).wait_send()
    returned(slice(0, HALVES), slice(0, CX), 0).wait_send()


def finish_kernel(total_ref, charges_ref, counts_ref, out_charges_ref, out_coords_ref):
    slot = lax.broadcasted_iota(jnp.int32, (1, SLOTS), 1)
    live = slot < counts_ref[0]
    out_charges_ref[...] = jnp.where(live, total_ref[0:1], 0.0)
    out_coords_ref[...] = jnp.where(live, charges_ref[...], 0.0) * total_ref[1:4]


def shape(dims, kind=FLOAT):
    return jax.ShapeDtypeStruct(dims, kind)


def per_device(charges, fractions, base_cells, counts, influence):
    tables = [jnp.asarray(t) for t in make_tables()]
    anywhere = pl.BlockSpec(memory_space=pltpu.HBM)
    vector = pl.BlockSpec(memory_space=pltpu.VMEM)
    scalar = pl.BlockSpec(memory_space=pltpu.SMEM)
    dma = pltpu.SemaphoreType.DMA
    charges = charges.reshape(1, SLOTS)
    total = pl.pallas_call(
        kernel,
        out_shape=shape((4, SLOTS)),
        in_specs=[vector, vector, vector, scalar] + [anywhere] * 5,
        out_specs=vector,
        scratch_shapes=[
            pltpu.VMEM((KX * WIDTH, CZ), FLOAT),
            pltpu.VMEM(tables[0].shape, HIGH_TYPE),
            pltpu.VMEM(tables[1].shape, HIGH_TYPE),
            pltpu.VMEM(tables[2].shape, HIGH_TYPE),
            pltpu.VMEM(tables[3].shape[1:], HIGH_TYPE),
            pltpu.VMEM((BLOCKS, 8, SLOTS), FLOAT),
            pltpu.VMEM((BLOCKS, ORDER, 8, SLOTS), FLOAT),
            pltpu.VMEM((BLOCKS, 3, 8, SLOTS), FLOAT),
            pltpu.VMEM((BLOCKS, 2, PATCH_Y, SLOTS), FLOAT),
            pltpu.VMEM((BLOCKS, 4 * CZ, SLOTS), HIGH_TYPE),
            pltpu.VMEM((BLOCKS, 2 * CZ, SLOTS), FLOAT),
            pltpu.VMEM((CX, KY + 8, CZ), FLOAT),
            pltpu.VMEM((HALVES, CX, ROWS, PART, CZ), FLOAT),
            pltpu.VMEM((HALVES, ROWS, CX, PART, CZ), FLOAT),
            pltpu.VMEM((HALVES, ROWS, CX, PART, CZ), FLOAT),
            pltpu.VMEM((HALVES, CX, ROWS, PART, CZ), FLOAT),
            pltpu.VMEM((BLOCKS, 4, SLOTS), FLOAT),
            pltpu.VMEM((BLOCKS, 4, SLOTS), FLOAT),
            dma((5,)),
            dma((4,)),
            dma((2,)),
            dma((HALVES,)),
            dma((HALVES - 1 + GATHER_GROUPS,)),
            dma,
        ],
        compiler_params=pltpu.CompilerParams(
            collective_id=0, has_side_effects=True, vmem_limit_bytes=VMEM_LIMIT
        ),
    )(charges, fractions, base_cells, counts, influence.reshape(KX * WIDTH, CZ), *tables)
    grad_charges, grad_coords = pl.pallas_call(
        finish_kernel,
        out_shape=(shape((1, SLOTS)), shape((3, SLOTS))),
        in_specs=[vector, vector, scalar],
        out_specs=(vector, vector),
        compiler_params=pltpu.CompilerParams(vmem_limit_bytes=VMEM_LIMIT),
    )(total, charges, counts)
    return grad_charges.reshape(SLOTS), grad_coords


def solution(mesh):
    return jax.shard_map(
        per_device,
        mesh=mesh,
        in_specs=(
            P(("row", "col")),
            P(None, ("row", "col")),
            P(None, ("row", "col")),
            P(("row", "col")),
            P(None, "row", "col"),
        ),
        out_specs=(P(("row", "col")), P(None, ("row", "col"))),
        check_vma=False,
    )
```

```python
import math

import jax
import jax.numpy as jnp
import ml_dtypes
import numpy as np
from jax import lax
from jax.experimental import pallas as pl
from jax.experimental.pallas import tpu as pltpu
from jax.sharding import PartitionSpec as P

KX = 384
KY = 256
KZ = 512
ORDER = 6
SLOTS = 512
ROWS = 64
COLS = 4
CX = KX // ROWS
CY = KY // COLS
CZ = KZ // COLS
PATCH_Y = 72
FINE = 8
COARSE = KZ // FINE
FAN = 2 * FINE
VMEM_LIMIT = 63 * 1024 * 1024
HALVES = 2
WIDTH = KY // ROWS
PART = WIDTH // HALVES
SIDES = 2
SIDE = ROWS // SIDES
BLOCKS = 2 * SIDES * COLS
MESH = pl.DeviceIdType.MESH

HIGH_TYPE = jnp.bfloat16
FLOAT = jnp.float32


def split_table(table):
    high = table.astype(np.float32).astype(ml_dtypes.bfloat16)
    low = (table - high.astype(np.float64)).astype(np.float32).astype(ml_dtypes.bfloat16)
    return high, low


def cas(product, length):
    angles = (product % length) * (2.0 * math.pi / length)
    return np.cos(angles) + np.sin(angles)


def make_tables():
    kx = np.arange(KX)
    table_x = np.zeros((2, KX + 8, KX), ml_dtypes.bfloat16)
    table_x[:, :KX] = split_table(cas(kx[:, None] * kx[None, :], KX))
    ky = np.arange(KY).reshape(SIDES, SIDE, HALVES, PART).transpose(0, 2, 1, 3)
    ky = ky.reshape(SIDES, KY // SIDES)
    y = np.arange(KY + 8)
    table_y = np.stack(split_table(cas(ky[:, :, None] * np.arange(KY), KY)), axis=1)
    table_y = np.pad(table_y, ((0, 0), (0, 0), (0, 8), (0, 0)))
    table_back = np.stack(split_table(cas(y[None, :, None] * ky[:, None, :], KY)), axis=1)
    kz = np.arange(KZ)
    coarse = (kz[:, None] * np.arange(COARSE)[None, :] * FINE % KZ) * (2.0 * math.pi / KZ)
    fine = kz[:, None] * np.arange(FAN)[None, :]
    table_z = np.zeros((COLS, 4 * CZ, 3 * FAN + 2 * COARSE), ml_dtypes.bfloat16)
    for place, values in ((0, np.cos(coarse)), (1, np.sin(coarse))):
        high, low = split_table(values)
        rows = slice(place * CZ, (place + 1) * CZ)
        table_z[:, rows, 3 * FAN : 3 * FAN + COARSE] = high.reshape(COLS, CZ, COARSE)
        table_z[:, rows, 3 * FAN + COARSE :] = low.reshape(COLS, CZ, COARSE)
    for place, values in ((2, cas(fine, KZ)), (3, cas(-fine, KZ))):
        high, low = split_table(values)
        rows = slice(place * CZ, (place + 1) * CZ)
        table_z[:, rows, :FAN] = high.reshape(COLS, CZ, FAN)
        table_z[:, rows, FAN : 2 * FAN] = high.reshape(COLS, CZ, FAN)
        table_z[:, rows, 2 * FAN : 3 * FAN] = low.reshape(COLS, CZ, FAN)
    return table_x, table_y, table_back, np.pad(table_z, ((0, 0), (0, 8), (0, 0)))


def spline_tables(fraction):
    previous = [fraction, 1.0 - fraction]
    fifth_order = previous
    for degree in range(3, 7):
        current = []
        for position in range(degree):
            summed = None
            if position < degree - 1:
                summed = (fraction + position) * previous[position]
            if position >= 1:
                second = (degree - fraction - position) * previous[position - 1]
                summed = second if summed is None else summed + second
            current.append(summed * (1.0 / (degree - 1)))
        fifth_order = previous
        previous = current
    slopes = []
    for position in range(6):
        if position == 0:
            slopes.append(fifth_order[0])
        elif position == 5:
            slopes.append(-fifth_order[4])
        else:
            slopes.append(fifth_order[position] - fifth_order[position - 1])
    return previous[::-1], slopes[::-1]


def split(value):
    high = value.astype(HIGH_TYPE)
    return high, (value - high.astype(FLOAT)).astype(HIGH_TYPE)


def dot(left, right, transposed=False):
    dims = (((1,), (1 if transposed else 0,)), ((), ()))
    return lax.dot_general(left, right, dims, preferred_element_type=FLOAT)


def dot3(left_high, left_low, right_high, right_low):
    return (
        dot(left_high, right_high) + dot(left_high, right_low) + dot(left_low, right_high)
    )


def dense(base, weights, rows):
    distance = lax.broadcasted_iota(jnp.int32, (rows, SLOTS), 0).astype(FLOAT) - base
    total = jnp.zeros((rows, SLOTS), FLOAT)
    for offset in range(ORDER):
        total = jnp.where(distance == offset, weights[offset], total)
    return total


def kernel(
    charges_ref,
    fractions_ref,
    cells_ref,
    counts_ref,
    influence_hbm,
    table_x_hbm,
    table_y_hbm,
    table_back_hbm,
    table_z_hbm,
    out_ref,
    influence_ref,
    table_x_ref,
    table_y_ref,
    table_back_ref,
    table_z_ref,
    atoms_ref,
    slope_ref,
    dense_x_ref,
    dense_y_ref,
    z_ref,
    turn_ref,
    acc_ref,
    send_ref,
    turned_ref,
    back_ref,
    returned_ref,
    partial_ref,
    arrived_ref,
    local_sems,
    send_sems,
    atoms_sems,
    turned_sems,
    returned_sems,
    arrived_sem,
):
    row = lax.axis_index("row")
    col = lax.axis_index("col")
    half_at = col // 2
    core = lax.rem(col, 2)
    side = row // SIDE
    place = lax.rem(row, SIDE)
    row_after = lax.rem(row + 1, ROWS)
    row_before = lax.rem(row + ROWS - 1, ROWS)

    def across(device_row):
        return lax.rem(device_row + SIDE, ROWS)

    sibling = half_at * 2 + 1 - core
    far_cols = [(1 - half_at) * 2 + core, (1 - half_at) * 2 + 1 - core]

    barrier = pltpu.get_barrier_semaphore()

    def greet(device_row, device_col):
        pl.semaphore_signal(
            barrier, inc=1, device_id=(device_row, device_col), device_id_type=MESH
        )

    others = [across(row)]
    for device_row in (row_after, row_before):
        others += [device_row, across(device_row)]
    for other in far_cols + [sibling]:
        greet(row, other)
    for other in far_cols + [sibling, col]:
        for device_row in others:
            greet(device_row, other)

    @pl.loop(1, SIDE)
    def _(step):
        greet(side * SIDE + lax.rem(place + step, SIDE), col)

    fetches = [
        pltpu.make_async_copy(table_z_hbm.at[col], table_z_ref, local_sems.at[0]),
        pltpu.make_async_copy(table_y_hbm.at[side], table_y_ref, local_sems.at[1]),
        pltpu.make_async_copy(table_x_hbm, table_x_ref, local_sems.at[2]),
        pltpu.make_async_copy(influence_hbm, influence_ref, local_sems.at[3]),
        pltpu.make_async_copy(table_back_hbm.at[side], table_back_ref, local_sems.at[4]),
    ]
    for fetch in fetches:
        fetch.start()

    slot = lax.broadcasted_iota(jnp.int32, (1, SLOTS), 1)
    own = side * 2 * COLS + col
    weight = jnp.where(slot < counts_ref[0], charges_ref[...], 0.0)
    atoms_ref[own, 0:1, :] = weight
    atoms_ref[own, 1:4, :] = fractions_ref[...]
    cells = cells_ref[...]
    atoms_ref[own, 4:5, :] = (cells[0:1] - row * CX).astype(FLOAT)
    atoms_ref[own, 5:6, :] = (cells[1:2] - col * CY).astype(FLOAT)
    atoms_ref[own, 6:7, :] = cells[2:3].astype(FLOAT)
    atoms_ref[own, 7:8, :] = weight
    acc_ref[...] = jnp.zeros(acc_ref.shape, FLOAT)

    def remote(source, target, send_sem, recv_sem, device_row, device_col):
        return pltpu.make_async_remote_copy(
            src_ref=source,
            dst_ref=target,
            send_sem=send_sem,
            recv_sem=recv_sem,
            device_id=(device_row, device_col),
            device_id_type=MESH,
        )

    def bases(index, behind):
        base_x = atoms_ref[index, 4:5, :] + float(CX) * (-behind)
        base_z = atoms_ref[index, 6:7, :]
        coarse = jnp.floor(base_z * (1.0 / FINE))
        return base_x, atoms_ref[index, 5:6, :], coarse, base_z - coarse * FINE

    def prepare(index, behind):
        values, slopes = spline_tables(atoms_ref[index, 1:4, :])
        for offset in range(ORDER):
            slope_ref[index, offset, 0:3, :] = slopes[offset]
        base_x, base_y, coarse, rest = bases(index, behind)

        def rows(dim):
            return [value[dim : dim + 1] for value in values]

        plain_x = dense(base_x, rows(0), 8)
        dense_x_ref[index, 0] = plain_x
        dense_x_ref[index, 2] = atoms_ref[index, 0:1, :] * plain_x
        dense_y_ref[index, 0] = dense(base_y, rows(1), PATCH_Y)
        hit = lax.broadcasted_iota(jnp.int32, (COARSE, SLOTS), 0).astype(FLOAT) == coarse
        hit = jnp.where(hit, 1.0, 0.0).astype(HIGH_TYPE)
        fine_high, fine_low = split(dense(rest, rows(2), FAN))
        joined = jnp.concatenate([fine_high, fine_low, fine_high, hit, hit], axis=0)
        parts = dot(table_z_ref[: 4 * CZ], joined)
        cosine, sine = parts[:CZ], parts[CZ : 2 * CZ]
        turn_ref[index, :CZ] = cosine
        turn_ref[index, CZ:] = sine
        wave = cosine * parts[2 * CZ : 3 * CZ] + sine * parts[3 * CZ :]
        wave_high, wave_low = split(wave)
        z_ref[index, 0:CZ] = wave_high
        z_ref[index, CZ : 2 * CZ] = wave_low

    def prepare_slopes(index, behind):
        base_x, base_y, coarse, rest = bases(index, behind)

        def rows(dim):
            return [slope_ref[index, offset, dim : dim + 1, :] for offset in range(ORDER)]

        dense_x_ref[index, 1] = dense(base_x, rows(0), 8)
        dense_y_ref[index, 1] = dense(base_y, rows(1), PATCH_Y)
        high, low = split(dense(rest, rows(2), FAN))
        joined = jnp.concatenate([high, low, high], axis=0)
        parts = dot(table_z_ref[2 * CZ : 4 * CZ, : 3 * FAN], joined)
        wave = turn_ref[index, :CZ] * parts[:CZ] + turn_ref[index, CZ:] * parts[CZ:]
        high, low = split(wave)
        z_ref[index, 2 * CZ : 3 * CZ] = high
        z_ref[index, 3 * CZ :] = low

    def block(member):
        here, behind, part = member
        return here * 2 * COLS + behind * COLS + part

    def spread(member):
        index = block(member)
        here, _, part = member
        plain_y = dense_y_ref[index, 0]
        patch = jnp.concatenate(
            [dense_x_ref[index, 2, x : x + 1, :] * plain_y for x in range(CX)], axis=0
        )
        high, low = split(patch)
        both = dot(high, z_ref[index, 0 : 2 * CZ], True)
        summed = both[:, :CZ] + both[:, CZ:] + dot(low, z_ref[index, 0:CZ], True)
        rows = pl.ds(pl.multiple_of(part * CY, CY), PATCH_Y)
        for x in range(CX):
            acc_ref[here * CX + x, rows, :] += summed[x * PATCH_Y : (x + 1) * PATCH_Y]

    away = 1 - side
    near = [(away, 0, col), (side, 0, sibling), (away, 0, sibling)]
    near += [(here, 1, part) for here in (side, away) for part in (col, sibling)]
    far = [
        (here, behind, part) for here in (side, away) for behind in range(2) for part in far_cols
    ]
    fetches[0].wait()
    prepare(own, 0)
    pl.semaphore_wait(barrier, 3 + 4 * 5 + SIDE - 1)

    for group, parts in ((0, far_cols), (1, [sibling, col])):
        for other in parts:
            for behind, device_row in enumerate((row, row_after)):
                slot_at = (device_row // SIDE) * 2 * COLS + behind * COLS + col
                for target in (device_row, across(device_row)):
                    if other is col and target is row:
                        continue
                    remote(
                        atoms_ref.at[own],
                        atoms_ref.at[slot_at],
                        send_sems.at[0],
                        atoms_sems.at[group],
                        target,
                        other,
                    ).start()
    spread((side, 0, col))
    for group, members in ((1, near), (0, far)):
        count = len(members)
        remote(
            atoms_ref.at[0:count],
            atoms_ref.at[0:count],
            send_sems.at[0],
            atoms_sems.at[group],
            row_after,
            col,
        ).wait_recv()
        for member in members:
            prepare(block(member), member[1])
        for member in members:
            spread(member)

    fetches[1].wait()
    for x in range(SIDES * CX):
        acc_ref[x, 0:8, :] += acc_ref[x, KY : KY + 8, :]
    depth = SIDE * PART
    send_flat = send_ref.reshape(HALVES, SIDES, CX, depth, CZ)
    fields = [
        split(jnp.concatenate([acc_ref[here * CX + x, :KY] for x in range(CX)], axis=1))
        for here in range(SIDES)
    ]
    for half in range(HALVES):
        rows = slice(half * depth, (half + 1) * depth)
        for here in range(SIDES):
            result = dot3(table_y_ref[0, rows], table_y_ref[1, rows], *fields[here])
            for x in range(CX):
                send_flat[half, here, x] = result[:, x * CZ : (x + 1) * CZ]

        @pl.loop(1, SIDE)
        def _(step):
            target = lax.rem(place + step, SIDE)
            remote(
                send_ref.at[half, :, :, target],
                turned_ref.at[half, :, place],
                send_sems.at[1],
                turned_sems.at[half],
                side * SIDE + target,
                col,
            ).start()

        turned_ref[half, :, place] = send_ref[half, :, :, place]

    for member in far + near + [(side, 0, col)]:
        prepare_slopes(block(member), member[1])
    fetches[2].wait()
    fetches[3].wait()
    back_flat = back_ref.reshape(HALVES, KX * PART, CZ)
    turned_flat = turned_ref.reshape(HALVES, KX * PART, CZ)
    for half in range(HALVES):
        influence = jnp.concatenate(
            [
                influence_ref[pl.ds(half * PART + j, KX, stride=WIDTH), :]
                for j in range(PART)
            ],
            axis=1,
        )
        remote(
            turned_ref.at[half, :, 0 : SIDE - 1],
            turned_ref.at[half, :, 0 : SIDE - 1],
            send_sems.at[1],
            turned_sems.at[half],
            row_after,
            col,
        ).wait_recv()
        field = jnp.concatenate(
            [turned_flat[half, pl.ds(j, KX, stride=PART), :] for j in range(PART)], axis=1
        )
        high, low = split(field)
        spectrum = influence * dot3(table_x_ref[0, :KX], table_x_ref[1, :KX], high, low)
        high, low = split(spectrum)
        result = dot3(table_x_ref[0, :KX], table_x_ref[1, :KX], high, low)
        for j in range(PART):
            back_flat[half, pl.ds(j, KX, stride=PART), :] = result[:, j * CZ : (j + 1) * CZ]

        @pl.loop(1, SIDE)
        def _(step):
            target = lax.rem(place + step, SIDE)
            remote(
                back_ref.at[half, :, target],
                returned_ref.at[half, :, :, place],
                send_sems.at[2],
                returned_sems.at[half],
                side * SIDE + target,
                col,
            ).start()

        returned_ref[half, :, :, place] = back_ref[half, :, place]

    fetches[4].wait()
    for half in range(HALVES):
        remote(
            returned_ref.at[half, :, :, 0 : SIDE - 1],
            returned_ref.at[half, :, :, 0 : SIDE - 1],
            send_sems.at[2],
            returned_sems.at[half],
            row_after,
            col,
        ).wait_recv()
    returned_flat = returned_ref.reshape(HALVES, SIDES, CX, depth, CZ)
    for here in range(SIDES):
        field = jnp.concatenate(
            [
                jnp.concatenate([returned_flat[half, here, x] for half in range(HALVES)], axis=0)
                for x in range(CX)
            ],
            axis=1,
        )
        high, low = split(field)
        result = dot3(table_back_ref[0], table_back_ref[1], high, low)
        for x in range(CX):
            acc_ref[here * CX + x] = result[:, x * CZ : (x + 1) * CZ]
    mine = (side, 0, col)
    for member in far + near + [mine]:
        here, behind, part = member
        index = block(member)
        plain_y = dense_y_ref[index, 0]
        slope_y = dense_y_ref[index, 1]
        rows = pl.ds(pl.multiple_of(part * CY, CY), PATCH_Y)
        patch = jnp.concatenate([acc_ref[here * CX + x, rows, :] for x in range(CX)], axis=0)
        high, low = split(patch)
        both = jnp.concatenate([high, low], axis=1)

        def contract(place_at):
            wave_high = z_ref[index, place_at * CZ : (place_at + 1) * CZ]
            wave_low = z_ref[index, (place_at + 1) * CZ : (place_at + 2) * CZ]
            twice = jnp.concatenate([wave_high, wave_high], axis=0)
            return dot(both, twice) + dot(high, wave_low)

        plain = contract(0)
        third = contract(2)
        sums = [0.0] * 4
        for x in range(CX):
            first_part = plain[x * PATCH_Y : (x + 1) * PATCH_Y]
            third_part = third[x * PATCH_Y : (x + 1) * PATCH_Y]
            inner = jnp.sum(plain_y * first_part, axis=0, keepdims=True)
            along_y = jnp.sum(slope_y * first_part, axis=0, keepdims=True)
            along_z = jnp.sum(plain_y * third_part, axis=0, keepdims=True)
            plain_x = dense_x_ref[index, 0, x : x + 1, :]
            slope_x = dense_x_ref[index, 1, x : x + 1, :]
            sums[0] = sums[0] + plain_x * inner
            sums[1] = sums[1] + slope_x * inner
            sums[2] = sums[2] + plain_x * along_y
            sums[3] = sums[3] + plain_x * along_z
        for k in range(4):
            partial_ref[index, k : k + 1] = sums[k]
        if member is not mine:
            remote(
                partial_ref.at[index],
                arrived_ref.at[behind * SIDES * COLS + side * COLS + col],
                send_sems.at[3],
                arrived_sem,
                lax.rem(here * SIDE + place + ROWS - behind, ROWS),
                part,
            ).start()

    arrived_ref[side * COLS + col] = partial_ref[own]
    remote(
        arrived_ref.at[0 : BLOCKS - 1],
        arrived_ref.at[0 : BLOCKS - 1],
        send_sems.at[3],
        arrived_sem,
        row_after,
        col,
    ).wait()
    total = arrived_ref[0]
    for index in range(1, BLOCKS):
        total = total + arrived_ref[index]
    out_ref[...] = total
    remote(
        atoms_ref.at[0 : BLOCKS - 1],
        atoms_ref.at[0 : BLOCKS - 1],
        send_sems.at[0],
        atoms_sems.at[0],
        row_after,
        col,
    ).wait_send()
    remote(
        turned_ref.at[:, :, 0 : SIDE - 1],
        turned_ref.at[:, :, 0 : SIDE - 1],
        send_sems.at[1],
        turned_sems.at[0],
        row_after,
        col,
    ).wait_send()
    remote(
        returned_ref.at[:, :, :, 0 : SIDE - 1],
        returned_ref.at[:, :, :, 0 : SIDE - 1],
        send_sems.at[2],
        returned_sems.at[0],
        row_after,
        col,
    ).wait_send()


def finish_kernel(total_ref, charges_ref, counts_ref, out_charges_ref, out_coords_ref):
    slot = lax.broadcasted_iota(jnp.int32, (1, SLOTS), 1)
    live = slot < counts_ref[0]
    out_charges_ref[...] = jnp.where(live, total_ref[0:1], 0.0)
    out_coords_ref[...] = jnp.where(live, charges_ref[...], 0.0) * total_ref[1:4]


def shape(dims, kind=FLOAT):
    return jax.ShapeDtypeStruct(dims, kind)


def per_device(charges, fractions, base_cells, counts, influence):
    tables = [jnp.asarray(t) for t in make_tables()]
    anywhere = pl.BlockSpec(memory_space=pltpu.HBM)
    vector = pl.BlockSpec(memory_space=pltpu.VMEM)
    scalar = pl.BlockSpec(memory_space=pltpu.SMEM)
    dma = pltpu.SemaphoreType.DMA
    charges = charges.reshape(1, SLOTS)
    total = pl.pallas_call(
        kernel,
        out_shape=shape((4, SLOTS)),
        in_specs=[vector, vector, vector, scalar] + [anywhere] * 5,
        out_specs=vector,
        scratch_shapes=[
            pltpu.VMEM((KX * WIDTH, CZ), FLOAT),
            pltpu.VMEM(tables[0].shape, HIGH_TYPE),
            pltpu.VMEM(tables[1].shape[1:], HIGH_TYPE),
            pltpu.VMEM(tables[2].shape[1:], HIGH_TYPE),
            pltpu.VMEM(tables[3].shape[1:], HIGH_TYPE),
            pltpu.VMEM((BLOCKS, 8, SLOTS), FLOAT),
            pltpu.VMEM((BLOCKS, ORDER, 8, SLOTS), FLOAT),
            pltpu.VMEM((BLOCKS, 3, 8, SLOTS), FLOAT),
            pltpu.VMEM((BLOCKS, 2, PATCH_Y, SLOTS), FLOAT),
            pltpu.VMEM((BLOCKS, 4 * CZ, SLOTS), HIGH_TYPE),
            pltpu.VMEM((BLOCKS, 2 * CZ, SLOTS), FLOAT),
            pltpu.VMEM((SIDES * CX, KY + 8, CZ), FLOAT),
            pltpu.VMEM((HALVES, SIDES, CX, SIDE, PART, CZ), FLOAT),
            pltpu.VMEM((HALVES, SIDES, SIDE, CX, PART, CZ), FLOAT),
            pltpu.VMEM((HALVES, SIDES, SIDE, CX, PART, CZ), FLOAT),
            pltpu.VMEM((HALVES, SIDES, CX, SIDE, PART, CZ), FLOAT),
            pltpu.VMEM((BLOCKS, 4, SLOTS), FLOAT),
            pltpu.VMEM((BLOCKS, 4, SLOTS), FLOAT),
            dma((5,)),
            dma((4,)),
            dma((2,)),
            dma((HALVES,)),
            dma((HALVES,)),
            dma,
        ],
        compiler_params=pltpu.CompilerParams(
            collective_id=0, has_side_effects=True, vmem_limit_bytes=VMEM_LIMIT
        ),
    )(charges, fractions, base_cells, counts, influence.reshape(KX * WIDTH, CZ), *tables)
    grad_charges, grad_coords = pl.pallas_call(
        finish_kernel,
        out_shape=(shape((1, SLOTS)), shape((3, SLOTS))),
        in_specs=[vector, vector, scalar],
        out_specs=(vector, vector),
        compiler_params=pltpu.CompilerParams(vmem_limit_bytes=VMEM_LIMIT),
    )(total, charges, counts)
    return grad_charges.reshape(SLOTS), grad_coords


def solution(mesh):
    return jax.shard_map(
        per_device,
        mesh=mesh,
        in_specs=(
            P(("row", "col")),
            P(None, ("row", "col")),
            P(None, ("row", "col")),
            P(("row", "col")),
            P(None, "row", "col"),
        ),
        out_specs=(P(("row", "col")), P(None, ("row", "col"))),
        check_vma=False,
    )
```

```python
import math

import jax
import jax.numpy as jnp
import ml_dtypes
import numpy as np
from jax import lax
from jax.experimental import pallas as pl
from jax.experimental.pallas import tpu as pltpu
from jax.sharding import PartitionSpec as P

KX = 384
KY = 256
KZ = 512
ORDER = 6
SLOTS = 512
ROWS = 64
COLS = 4
CX = KX // ROWS
CY = KY // COLS
CZ = KZ // COLS
PATCH_Y = 72
FINE = 8
COARSE = KZ // FINE
FAN = 2 * FINE
VMEM_LIMIT = 63 * 1024 * 1024
HALVES = 2
WIDTH = KY // ROWS
PART = WIDTH // HALVES
SIDES = 2
SIDE = ROWS // SIDES
BLOCKS = 2 * SIDES * COLS
MESH = pl.DeviceIdType.MESH

HIGH_TYPE = jnp.bfloat16
FLOAT = jnp.float32


def split_table(table):
    high = table.astype(np.float32).astype(ml_dtypes.bfloat16)
    low = (table - high.astype(np.float64)).astype(np.float32).astype(ml_dtypes.bfloat16)
    return high, low


def cas(product, length):
    angles = (product % length) * (2.0 * math.pi / length)
    return np.cos(angles) + np.sin(angles)


def make_tables():
    kx = np.arange(KX)
    table_x = np.zeros((2, KX + 8, KX), ml_dtypes.bfloat16)
    table_x[:, :KX] = split_table(cas(kx[:, None] * kx[None, :], KX))
    ky = np.arange(KY).reshape(SIDES, SIDE, HALVES, PART).transpose(0, 2, 1, 3)
    ky = ky.reshape(SIDES, KY // SIDES)
    y = np.arange(KY + 8)
    table_y = np.stack(split_table(cas(ky[:, :, None] * np.arange(KY), KY)), axis=1)
    table_y = np.pad(table_y, ((0, 0), (0, 0), (0, 8), (0, 0)))
    table_back = np.stack(split_table(cas(y[None, :, None] * ky[:, None, :], KY)), axis=1)
    kz = np.arange(KZ)
    coarse = (kz[:, None] * np.arange(COARSE)[None, :] * FINE % KZ) * (2.0 * math.pi / KZ)
    fine = kz[:, None] * np.arange(FAN)[None, :]
    table_z = np.zeros((COLS, 4 * CZ, 3 * FAN + 2 * COARSE), ml_dtypes.bfloat16)
    for place, values in ((0, np.cos(coarse)), (1, np.sin(coarse))):
        high, low = split_table(values)
        rows = slice(place * CZ, (place + 1) * CZ)
        table_z[:, rows, 3 * FAN : 3 * FAN + COARSE] = high.reshape(COLS, CZ, COARSE)
        table_z[:, rows, 3 * FAN + COARSE :] = low.reshape(COLS, CZ, COARSE)
    for place, values in ((2, cas(fine, KZ)), (3, cas(-fine, KZ))):
        high, low = split_table(values)
        rows = slice(place * CZ, (place + 1) * CZ)
        table_z[:, rows, :FAN] = high.reshape(COLS, CZ, FAN)
        table_z[:, rows, FAN : 2 * FAN] = high.reshape(COLS, CZ, FAN)
        table_z[:, rows, 2 * FAN : 3 * FAN] = low.reshape(COLS, CZ, FAN)
    return table_x, table_y, table_back, np.pad(table_z, ((0, 0), (0, 8), (0, 0)))


def spline_tables(fraction):
    previous = [fraction, 1.0 - fraction]
    fifth_order = previous
    for degree in range(3, 7):
        current = []
        for position in range(degree):
            summed = None
            if position < degree - 1:
                summed = (fraction + position) * previous[position]
            if position >= 1:
                second = (degree - fraction - position) * previous[position - 1]
                summed = second if summed is None else summed + second
            current.append(summed * (1.0 / (degree - 1)))
        fifth_order = previous
        previous = current
    slopes = []
    for position in range(6):
        if position == 0:
            slopes.append(fifth_order[0])
        elif position == 5:
            slopes.append(-fifth_order[4])
        else:
            slopes.append(fifth_order[position] - fifth_order[position - 1])
    return previous[::-1], slopes[::-1]


def split(value):
    high = value.astype(HIGH_TYPE)
    return high, (value - high.astype(FLOAT)).astype(HIGH_TYPE)


def dot(left, right, transposed=False):
    dims = (((1,), (1 if transposed else 0,)), ((), ()))
    return lax.dot_general(left, right, dims, preferred_element_type=FLOAT)


def dot3(left_high, left_low, right_high, right_low):
    return (
        dot(left_high, right_high) + dot(left_high, right_low) + dot(left_low, right_high)
    )


def dense(base, weights, rows):
    distance = lax.broadcasted_iota(jnp.int32, (rows, SLOTS), 0).astype(FLOAT) - base
    total = jnp.zeros((rows, SLOTS), FLOAT)
    for offset in range(ORDER):
        total = jnp.where(distance == offset, weights[offset], total)
    return total


def kernel(
    charges_ref,
    fractions_ref,
    cells_ref,
    counts_ref,
    influence_hbm,
    table_x_hbm,
    table_y_hbm,
    table_back_hbm,
    table_z_hbm,
    out_ref,
    influence_ref,
    table_x_ref,
    table_y_ref,
    table_back_ref,
    table_z_ref,
    atoms_ref,
    slope_ref,
    dense_x_ref,
    dense_y_ref,
    z_ref,
    turn_ref,
    acc_ref,
    send_ref,
    turned_ref,
    back_ref,
    returned_ref,
    partial_ref,
    arrived_ref,
    local_sems,
    send_sems,
    atoms_sems,
    turned_sems,
    returned_sems,
    arrived_sem,
):
    row = lax.axis_index("row")
    col = lax.axis_index("col")
    half_at = col // 2
    core = lax.rem(col, 2)
    side = row // SIDE
    place = lax.rem(row, SIDE)
    row_after = lax.rem(row + 1, ROWS)
    row_before = lax.rem(row + ROWS - 1, ROWS)

    def across(device_row):
        return lax.rem(device_row + SIDE, ROWS)

    sibling = half_at * 2 + 1 - core
    far_cols = [(1 - half_at) * 2 + core, (1 - half_at) * 2 + 1 - core]

    barrier = pltpu.get_barrier_semaphore()

    def greet(device_row, device_col):
        pl.semaphore_signal(
            barrier, inc=1, device_id=(device_row, device_col), device_id_type=MESH
        )

    others = [across(row)]
    for device_row in (row_after, row_before):
        others += [device_row, across(device_row)]
    for other in far_cols + [sibling]:
        greet(row, other)
    for other in far_cols + [sibling, col]:
        for device_row in others:
            greet(device_row, other)

    @pl.loop(1, SIDE)
    def _(step):
        greet(side * SIDE + lax.rem(place + step, SIDE), col)

    fetches = [
        pltpu.make_async_copy(table_z_hbm.at[col], table_z_ref, local_sems.at[0]),
        pltpu.make_async_copy(table_y_hbm.at[side], table_y_ref, local_sems.at[1]),
        pltpu.make_async_copy(table_x_hbm, table_x_ref, local_sems.at[2]),
        pltpu.make_async_copy(influence_hbm, influence_ref, local_sems.at[3]),
        pltpu.make_async_copy(table_back_hbm.at[side], table_back_ref, local_sems.at[4]),
    ]
    for fetch in fetches:
        fetch.start()

    slot = lax.broadcasted_iota(jnp.int32, (1, SLOTS), 1)
    own = side * 2 * COLS + col
    weight = jnp.where(slot < counts_ref[0], charges_ref[...], 0.0)
    atoms_ref[own, 0:1, :] = weight
    atoms_ref[own, 1:4, :] = fractions_ref[...]
    cells = cells_ref[...]
    atoms_ref[own, 4:5, :] = (cells[0:1] - row * CX).astype(FLOAT)
    atoms_ref[own, 5:6, :] = (cells[1:2] - col * CY).astype(FLOAT)
    atoms_ref[own, 6:7, :] = cells[2:3].astype(FLOAT)
    atoms_ref[own, 7:8, :] = weight
    acc_ref[...] = jnp.zeros(acc_ref.shape, FLOAT)

    def remote(source, target, send_sem, recv_sem, device_row, device_col):
        return pltpu.make_async_remote_copy(
            src_ref=source,
            dst_ref=target,
            send_sem=send_sem,
            recv_sem=recv_sem,
            device_id=(device_row, device_col),
            device_id_type=MESH,
        )

    def bases(index, behind):
        base_x = atoms_ref[index, 4:5, :] + float(CX) * (-behind)
        base_z = atoms_ref[index, 6:7, :]
        coarse = jnp.floor(base_z * (1.0 / FINE))
        return base_x, atoms_ref[index, 5:6, :], coarse, base_z - coarse * FINE

    def prepare(index, behind):
        values, slopes = spline_tables(atoms_ref[index, 1:4, :])
        for offset in range(ORDER):
            slope_ref[index, offset, 0:3, :] = slopes[offset]
        base_x, base_y, coarse, rest = bases(index, behind)

        def rows(dim):
            return [value[dim : dim + 1] for value in values]

        plain_x = dense(base_x, rows(0), 8)
        dense_x_ref[index, 0] = plain_x
        dense_x_ref[index, 2] = atoms_ref[index, 0:1, :] * plain_x
        dense_y_ref[index, 0] = dense(base_y, rows(1), PATCH_Y)
        hit = lax.broadcasted_iota(jnp.int32, (COARSE, SLOTS), 0).astype(FLOAT) == coarse
        hit = jnp.where(hit, 1.0, 0.0).astype(HIGH_TYPE)
        fine_high, fine_low = split(dense(rest, rows(2), FAN))
        joined = jnp.concatenate([fine_high, fine_low, fine_high, hit, hit], axis=0)
        parts = dot(table_z_ref[: 4 * CZ], joined)
        cosine, sine = parts[:CZ], parts[CZ : 2 * CZ]
        turn_ref[index, :CZ] = cosine
        turn_ref[index, CZ:] = sine
        wave = cosine * parts[2 * CZ : 3 * CZ] + sine * parts[3 * CZ :]
        wave_high, wave_low = split(wave)
        z_ref[index, 0:CZ] = wave_high
        z_ref[index, CZ : 2 * CZ] = wave_low

    def prepare_slopes(index, behind):
        base_x, base_y, coarse, rest = bases(index, behind)

        def rows(dim):
            return [slope_ref[index, offset, dim : dim + 1, :] for offset in range(ORDER)]

        dense_x_ref[index, 1] = dense(base_x, rows(0), 8)
        dense_y_ref[index, 1] = dense(base_y, rows(1), PATCH_Y)
        high, low = split(dense(rest, rows(2), FAN))
        joined = jnp.concatenate([high, low, high], axis=0)
        parts = dot(table_z_ref[2 * CZ : 4 * CZ, : 3 * FAN], joined)
        wave = turn_ref[index, :CZ] * parts[:CZ] + turn_ref[index, CZ:] * parts[CZ:]
        high, low = split(wave)
        z_ref[index, 2 * CZ : 3 * CZ] = high
        z_ref[index, 3 * CZ :] = low

    def block(member):
        here, behind, part = member
        return here * 2 * COLS + behind * COLS + part

    def spread(member):
        index = block(member)
        here, _, part = member
        plain_y = dense_y_ref[index, 0]
        patch = jnp.concatenate(
            [dense_x_ref[index, 2, x : x + 1, :] * plain_y for x in range(CX)], axis=0
        )
        high, low = split(patch)
        both = dot(high, z_ref[index, 0 : 2 * CZ], True)
        summed = both[:, :CZ] + both[:, CZ:] + dot(low, z_ref[index, 0:CZ], True)
        rows = pl.ds(pl.multiple_of(part * CY, CY), PATCH_Y)
        for x in range(CX):
            acc_ref[here * CX + x, rows, :] += summed[x * PATCH_Y : (x + 1) * PATCH_Y]

    away = 1 - side
    near = [(away, 0, col), (side, 0, sibling), (away, 0, sibling)]
    near += [(here, 1, part) for here in (side, away) for part in (col, sibling)]
    far = [
        (here, behind, part) for here in (side, away) for behind in range(2) for part in far_cols
    ]
    fetches[0].wait()
    prepare(own, 0)
    pl.semaphore_wait(barrier, 3 + 4 * 5 + SIDE - 1)

    for group, parts in ((0, far_cols), (1, [sibling, col])):
        for other in parts:
            for behind, device_row in enumerate((row, row_after)):
                slot_at = (device_row // SIDE) * 2 * COLS + behind * COLS + col
                for target in (device_row, across(device_row)):
                    if other is col and target is row:
                        continue
                    remote(
                        atoms_ref.at[own],
                        atoms_ref.at[slot_at],
                        send_sems.at[0],
                        atoms_sems.at[group],
                        target,
                        other,
                    ).start()
    spread((side, 0, col))
    depth = SIDE * PART
    send_flat = send_ref.reshape(HALVES, SIDES, CX, depth, CZ)

    def arrive(group, count):
        remote(
            atoms_ref.at[0:count],
            atoms_ref.at[0:count],
            send_sems.at[0],
            atoms_sems.at[group],
            row_after,
            col,
        ).wait_recv()

    def work(members):
        for member in members:
            prepare(block(member), member[1])
        for member in members:
            spread(member)

    arrive(1, len(near))
    work(near)
    arrive(0, len(far))
    for here in (away, side):
        work([member for member in far if member[0] is here])
        if here is away:
            fetches[1].wait()
        for x in range(CX):
            acc_ref[here * CX + x, 0:8, :] += acc_ref[here * CX + x, KY : KY + 8, :]
        field = split(jnp.concatenate([acc_ref[here * CX + x, :KY] for x in range(CX)], axis=1))
        for half in range(HALVES):
            rows = slice(half * depth, (half + 1) * depth)
            result = dot3(table_y_ref[0, rows], table_y_ref[1, rows], *field)
            for x in range(CX):
                send_flat[half, here, x] = result[:, x * CZ : (x + 1) * CZ]

            @pl.loop(1, SIDE)
            def _(step):
                target = lax.rem(place + step, SIDE)
                remote(
                    send_ref.at[half, here, :, target],
                    turned_ref.at[half, here, place],
                    send_sems.at[1],
                    turned_sems.at[half],
                    side * SIDE + target,
                    col,
                ).start()

    for half in range(HALVES):
        turned_ref[half, :, place] = send_ref[half, :, :, place]

    for member in far + near + [(side, 0, col)]:
        prepare_slopes(block(member), member[1])
    fetches[2].wait()
    fetches[3].wait()
    back_flat = back_ref.reshape(HALVES, KX * PART, CZ)
    turned_flat = turned_ref.reshape(HALVES, KX * PART, CZ)
    for half in range(HALVES):
        influence = jnp.concatenate(
            [
                influence_ref[pl.ds(half * PART + j, KX, stride=WIDTH), :]
                for j in range(PART)
            ],
            axis=1,
        )
        remote(
            turned_ref.at[half, :, 0 : SIDE - 1],
            turned_ref.at[half, :, 0 : SIDE - 1],
            send_sems.at[1],
            turned_sems.at[half],
            row_after,
            col,
        ).wait_recv()
        field = jnp.concatenate(
            [turned_flat[half, pl.ds(j, KX, stride=PART), :] for j in range(PART)], axis=1
        )
        high, low = split(field)
        spectrum = influence * dot3(table_x_ref[0, :KX], table_x_ref[1, :KX], high, low)
        high, low = split(spectrum)
        result = dot3(table_x_ref[0, :KX], table_x_ref[1, :KX], high, low)
        for j in range(PART):
            back_flat[half, pl.ds(j, KX, stride=PART), :] = result[:, j * CZ : (j + 1) * CZ]

        if half < HALVES - 1:
            pieces = [slice(0, SIDES)]
        else:
            pieces = [away, side]
        for number, here in enumerate(pieces):

            @pl.loop(1, SIDE)
            def _(step):
                target = lax.rem(place + step, SIDE)
                source = back_ref.at[half, here, target]
                landing = returned_ref.at[half, here, :, place]
                remote(
                    source,
                    landing,
                    send_sems.at[2],
                    returned_sems.at[half + number],
                    side * SIDE + target,
                    col,
                ).start()

        returned_ref[half, :, :, place] = back_ref[half, :, place]

    fetches[4].wait()
    def returned(half, here, number):
        remote(
            returned_ref.at[half, here, :, 0 : SIDE - 1],
            returned_ref.at[half, here, :, 0 : SIDE - 1],
            send_sems.at[2],
            returned_sems.at[number],
            row_after,
            col,
        ).wait_recv()

    for half in range(HALVES - 1):
        returned(half, slice(0, SIDES), half)
    returned_flat = returned_ref.reshape(HALVES, SIDES, CX, depth, CZ)
    mine = (side, 0, col)

    def collect(number, here):
        returned(HALVES - 1, here, HALVES - 1 + number)
        field = jnp.concatenate(
            [
                jnp.concatenate([returned_flat[half, here, x] for half in range(HALVES)], axis=0)
                for x in range(CX)
            ],
            axis=1,
        )
        high, low = split(field)
        result = dot3(table_back_ref[0], table_back_ref[1], high, low)
        for x in range(CX):
            acc_ref[here * CX + x] = result[:, x * CZ : (x + 1) * CZ]
    def contribute(member):
        here, behind, part = member
        index = block(member)
        plain_y = dense_y_ref[index, 0]
        slope_y = dense_y_ref[index, 1]
        rows = pl.ds(pl.multiple_of(part * CY, CY), PATCH_Y)
        patch = jnp.concatenate([acc_ref[here * CX + x, rows, :] for x in range(CX)], axis=0)
        high, low = split(patch)
        both = jnp.concatenate([high, low], axis=1)

        def contract(place_at):
            wave_high = z_ref[index, place_at * CZ : (place_at + 1) * CZ]
            wave_low = z_ref[index, (place_at + 1) * CZ : (place_at + 2) * CZ]
            twice = jnp.concatenate([wave_high, wave_high], axis=0)
            return dot(both, twice) + dot(high, wave_low)

        plain = contract(0)
        third = contract(2)
        sums = [0.0] * 4
        for x in range(CX):
            first_part = plain[x * PATCH_Y : (x + 1) * PATCH_Y]
            third_part = third[x * PATCH_Y : (x + 1) * PATCH_Y]
            inner = jnp.sum(plain_y * first_part, axis=0, keepdims=True)
            along_y = jnp.sum(slope_y * first_part, axis=0, keepdims=True)
            along_z = jnp.sum(plain_y * third_part, axis=0, keepdims=True)
            plain_x = dense_x_ref[index, 0, x : x + 1, :]
            slope_x = dense_x_ref[index, 1, x : x + 1, :]
            sums[0] = sums[0] + plain_x * inner
            sums[1] = sums[1] + slope_x * inner
            sums[2] = sums[2] + plain_x * along_y
            sums[3] = sums[3] + plain_x * along_z
        for k in range(4):
            partial_ref[index, k : k + 1] = sums[k]
        if member is not mine:
            remote(
                partial_ref.at[index],
                arrived_ref.at[behind * SIDES * COLS + side * COLS + col],
                send_sems.at[3],
                arrived_sem,
                lax.rem(here * SIDE + place + ROWS - behind, ROWS),
                part,
            ).start()

    for number, here in enumerate((away, side)):
        collect(number, here)
        members = [member for member in far + near if member[0] is here]
        if here is side:
            members.append(mine)
        for member in members:
            contribute(member)

    arrived_ref[side * COLS + col] = partial_ref[own]
    remote(
        arrived_ref.at[0 : BLOCKS - 1],
        arrived_ref.at[0 : BLOCKS - 1],
        send_sems.at[3],
        arrived_sem,
        row_after,
        col,
    ).wait()
    total = arrived_ref[0]
    for index in range(1, BLOCKS):
        total = total + arrived_ref[index]
    out_ref[...] = total
    remote(
        atoms_ref.at[0 : BLOCKS - 1],
        atoms_ref.at[0 : BLOCKS - 1],
        send_sems.at[0],
        atoms_sems.at[0],
        row_after,
        col,
    ).wait_send()
    remote(
        turned_ref.at[:, :, 0 : SIDE - 1],
        turned_ref.at[:, :, 0 : SIDE - 1],
        send_sems.at[1],
        turned_sems.at[0],
        row_after,
        col,
    ).wait_send()
    remote(
        returned_ref.at[:, :, :, 0 : SIDE - 1],
        returned_ref.at[:, :, :, 0 : SIDE - 1],
        send_sems.at[2],
        returned_sems.at[0],
        row_after,
        col,
    ).wait_send()


def finish_kernel(total_ref, charges_ref, counts_ref, out_charges_ref, out_coords_ref):
    slot = lax.broadcasted_iota(jnp.int32, (1, SLOTS), 1)
    live = slot < counts_ref[0]
    out_charges_ref[...] = jnp.where(live, total_ref[0:1], 0.0)
    out_coords_ref[...] = jnp.where(live, charges_ref[...], 0.0) * total_ref[1:4]


def shape(dims, kind=FLOAT):
    return jax.ShapeDtypeStruct(dims, kind)


def per_device(charges, fractions, base_cells, counts, influence):
    tables = [jnp.asarray(t) for t in make_tables()]
    anywhere = pl.BlockSpec(memory_space=pltpu.HBM)
    vector = pl.BlockSpec(memory_space=pltpu.VMEM)
    scalar = pl.BlockSpec(memory_space=pltpu.SMEM)
    dma = pltpu.SemaphoreType.DMA
    charges = charges.reshape(1, SLOTS)
    total = pl.pallas_call(
        kernel,
        out_shape=shape((4, SLOTS)),
        in_specs=[vector, vector, vector, scalar] + [anywhere] * 5,
        out_specs=vector,
        scratch_shapes=[
            pltpu.VMEM((KX * WIDTH, CZ), FLOAT),
            pltpu.VMEM(tables[0].shape, HIGH_TYPE),
            pltpu.VMEM(tables[1].shape[1:], HIGH_TYPE),
            pltpu.VMEM(tables[2].shape[1:], HIGH_TYPE),
            pltpu.VMEM(tables[3].shape[1:], HIGH_TYPE),
            pltpu.VMEM((BLOCKS, 8, SLOTS), FLOAT),
            pltpu.VMEM((BLOCKS, ORDER, 8, SLOTS), FLOAT),
            pltpu.VMEM((BLOCKS, 3, 8, SLOTS), FLOAT),
            pltpu.VMEM((BLOCKS, 2, PATCH_Y, SLOTS), FLOAT),
            pltpu.VMEM((BLOCKS, 4 * CZ, SLOTS), HIGH_TYPE),
            pltpu.VMEM((BLOCKS, 2 * CZ, SLOTS), FLOAT),
            pltpu.VMEM((SIDES * CX, KY + 8, CZ), FLOAT),
            pltpu.VMEM((HALVES, SIDES, CX, SIDE, PART, CZ), FLOAT),
            pltpu.VMEM((HALVES, SIDES, SIDE, CX, PART, CZ), FLOAT),
            pltpu.VMEM((HALVES, SIDES, SIDE, CX, PART, CZ), FLOAT),
            pltpu.VMEM((HALVES, SIDES, CX, SIDE, PART, CZ), FLOAT),
            pltpu.VMEM((BLOCKS, 4, SLOTS), FLOAT),
            pltpu.VMEM((BLOCKS, 4, SLOTS), FLOAT),
            dma((5,)),
            dma((4,)),
            dma((2,)),
            dma((HALVES,)),
            dma((HALVES + SIDES - 1,)),
            dma,
        ],
        compiler_params=pltpu.CompilerParams(
            collective_id=0, has_side_effects=True, vmem_limit_bytes=VMEM_LIMIT
        ),
    )(charges, fractions, base_cells, counts, influence.reshape(KX * WIDTH, CZ), *tables)
    grad_charges, grad_coords = pl.pallas_call(
        finish_kernel,
        out_shape=(shape((1, SLOTS)), shape((3, SLOTS))),
        in_specs=[vector, vector, scalar],
        out_specs=(vector, vector),
        compiler_params=pltpu.CompilerParams(vmem_limit_bytes=VMEM_LIMIT),
    )(total, charges, counts)
    return grad_charges.reshape(SLOTS), grad_coords


def solution(mesh):
    return jax.shard_map(
        per_device,
        mesh=mesh,
        in_specs=(
            P(("row", "col")),
            P(None, ("row", "col")),
            P(None, ("row", "col")),
            P(("row", "col")),
            P(None, "row", "col"),
        ),
        out_specs=(P(("row", "col")), P(None, ("row", "col"))),
        check_vma=False,
    )
```

```python
import math

import jax
import jax.numpy as jnp
import ml_dtypes
import numpy as np
from jax import lax
from jax.experimental import pallas as pl
from jax.experimental.pallas import tpu as pltpu
from jax.sharding import PartitionSpec as P

KX = 384
KY = 256
KZ = 512
ORDER = 6
SLOTS = 512
ROWS = 64
COLS = 4
CX = KX // ROWS
CY = KY // COLS
CZ = KZ // COLS
PATCH_Y = 72
FINE = 8
COARSE = KZ // FINE
FAN = 2 * FINE
VMEM_LIMIT = 63 * 1024 * 1024
HALVES = 2
WIDTH = KY // ROWS
PART = WIDTH // HALVES
SIDES = 2
SIDE = ROWS // SIDES
BLOCKS = 2 * SIDES * COLS
MESH = pl.DeviceIdType.MESH

HIGH_TYPE = jnp.bfloat16
FLOAT = jnp.float32


def split_table(table):
    high = table.astype(np.float32).astype(ml_dtypes.bfloat16)
    low = (table - high.astype(np.float64)).astype(np.float32).astype(ml_dtypes.bfloat16)
    return high, low


def cas(product, length):
    angles = (product % length) * (2.0 * math.pi / length)
    return np.cos(angles) + np.sin(angles)


def make_tables():
    kx = np.arange(KX)
    table_x = np.zeros((2, KX + 8, KX), ml_dtypes.bfloat16)
    table_x[:, :KX] = split_table(cas(kx[:, None] * kx[None, :], KX))
    ky = np.arange(KY).reshape(SIDES, SIDE, HALVES, PART).transpose(0, 2, 1, 3)
    ky = ky.reshape(SIDES, KY // SIDES)
    y = np.arange(KY + 8)
    table_y = np.stack(split_table(cas(ky[:, :, None] * np.arange(KY), KY)), axis=1)
    table_y = np.pad(table_y, ((0, 0), (0, 0), (0, 8), (0, 0)))
    table_back = np.stack(split_table(cas(y[None, :, None] * ky[:, None, :], KY)), axis=1)
    kz = np.arange(KZ)
    coarse = (kz[:, None] * np.arange(COARSE)[None, :] * FINE % KZ) * (2.0 * math.pi / KZ)
    fine = kz[:, None] * np.arange(FAN)[None, :]
    table_z = np.zeros((COLS, 4 * CZ, 3 * FAN + 2 * COARSE), ml_dtypes.bfloat16)
    for place, values in ((0, np.cos(coarse)), (1, np.sin(coarse))):
        high, low = split_table(values)
        rows = slice(place * CZ, (place + 1) * CZ)
        table_z[:, rows, 3 * FAN : 3 * FAN + COARSE] = high.reshape(COLS, CZ, COARSE)
        table_z[:, rows, 3 * FAN + COARSE :] = low.reshape(COLS, CZ, COARSE)
    for place, values in ((2, cas(fine, KZ)), (3, cas(-fine, KZ))):
        high, low = split_table(values)
        rows = slice(place * CZ, (place + 1) * CZ)
        table_z[:, rows, :FAN] = high.reshape(COLS, CZ, FAN)
        table_z[:, rows, FAN : 2 * FAN] = high.reshape(COLS, CZ, FAN)
        table_z[:, rows, 2 * FAN : 3 * FAN] = low.reshape(COLS, CZ, FAN)
    return table_x, table_y, table_back, np.pad(table_z, ((0, 0), (0, 8), (0, 0)))


def spline_tables(fraction):
    previous = [fraction, 1.0 - fraction]
    fifth_order = previous
    for degree in range(3, 7):
        current = []
        for position in range(degree):
            summed = None
            if position < degree - 1:
                summed = (fraction + position) * previous[position]
            if position >= 1:
                second = (degree - fraction - position) * previous[position - 1]
                summed = second if summed is None else summed + second
            current.append(summed * (1.0 / (degree - 1)))
        fifth_order = previous
        previous = current
    slopes = []
    for position in range(6):
        if position == 0:
            slopes.append(fifth_order[0])
        elif position == 5:
            slopes.append(-fifth_order[4])
        else:
            slopes.append(fifth_order[position] - fifth_order[position - 1])
    return previous[::-1], slopes[::-1]


def split(value):
    high = value.astype(HIGH_TYPE)
    return high, (value - high.astype(FLOAT)).astype(HIGH_TYPE)


def dot(left, right, transposed=False):
    dims = (((1,), (1 if transposed else 0,)), ((), ()))
    return lax.dot_general(left, right, dims, preferred_element_type=FLOAT)


def dot3(left_high, left_low, right_high, right_low):
    return (
        dot(left_high, right_high) + dot(left_high, right_low) + dot(left_low, right_high)
    )


def dense(base, weights, rows):
    distance = lax.broadcasted_iota(jnp.int32, (rows, SLOTS), 0).astype(FLOAT) - base
    total = jnp.zeros((rows, SLOTS), FLOAT)
    for offset in range(ORDER):
        total = jnp.where(distance == offset, weights[offset], total)
    return total


def kernel(
    charges_ref,
    fractions_ref,
    cells_ref,
    counts_ref,
    influence_hbm,
    table_x_hbm,
    table_y_hbm,
    table_back_hbm,
    table_z_hbm,
    out_ref,
    influence_ref,
    table_x_ref,
    table_y_ref,
    table_back_ref,
    table_z_ref,
    atoms_ref,
    slope_ref,
    dense_x_ref,
    dense_y_ref,
    z_ref,
    turn_ref,
    acc_ref,
    send_ref,
    turned_ref,
    back_ref,
    returned_ref,
    partial_ref,
    arrived_ref,
    local_sems,
    send_sems,
    atoms_sems,
    turned_sems,
    returned_sems,
    arrived_sem,
):
    row = lax.axis_index("row")
    col = lax.axis_index("col")
    half_at = col // 2
    core = lax.rem(col, 2)
    side = row // SIDE
    place = lax.rem(row, SIDE)
    row_after = lax.rem(row + 1, ROWS)
    row_before = lax.rem(row + ROWS - 1, ROWS)

    def across(device_row):
        return lax.rem(device_row + SIDE, ROWS)

    sibling = half_at * 2 + 1 - core
    far_cols = [(1 - half_at) * 2 + core, (1 - half_at) * 2 + 1 - core]

    barrier = pltpu.get_barrier_semaphore()

    def greet(device_row, device_col):
        pl.semaphore_signal(
            barrier, inc=1, device_id=(device_row, device_col), device_id_type=MESH
        )

    others = [across(row)]
    for device_row in (row_after, row_before):
        others += [device_row, across(device_row)]
    for other in far_cols + [sibling]:
        greet(row, other)
    for other in far_cols + [sibling, col]:
        for device_row in others:
            greet(device_row, other)

    @pl.loop(1, SIDE)
    def _(step):
        greet(side * SIDE + lax.rem(place + step, SIDE), col)

    fetches = [
        pltpu.make_async_copy(table_z_hbm.at[col], table_z_ref, local_sems.at[0]),
        pltpu.make_async_copy(table_y_hbm.at[side], table_y_ref, local_sems.at[1]),
        pltpu.make_async_copy(table_x_hbm, table_x_ref, local_sems.at[2]),
        pltpu.make_async_copy(influence_hbm, influence_ref, local_sems.at[3]),
        pltpu.make_async_copy(table_back_hbm.at[side], table_back_ref, local_sems.at[4]),
    ]
    for fetch in fetches:
        fetch.start()

    slot = lax.broadcasted_iota(jnp.int32, (1, SLOTS), 1)
    own = side * 2 * COLS + col
    weight = jnp.where(slot < counts_ref[0], charges_ref[...], 0.0)
    atoms_ref[own, 0:1, :] = weight
    atoms_ref[own, 1:4, :] = fractions_ref[...]
    cells = cells_ref[...]
    atoms_ref[own, 4:5, :] = (cells[0:1] - row * CX).astype(FLOAT)
    atoms_ref[own, 5:6, :] = (cells[1:2] - col * CY).astype(FLOAT)
    atoms_ref[own, 6:7, :] = cells[2:3].astype(FLOAT)
    atoms_ref[own, 7:8, :] = weight
    acc_ref[...] = jnp.zeros(acc_ref.shape, FLOAT)

    def remote(source, target, send_sem, recv_sem, device_row, device_col):
        return pltpu.make_async_remote_copy(
            src_ref=source,
            dst_ref=target,
            send_sem=send_sem,
            recv_sem=recv_sem,
            device_id=(device_row, device_col),
            device_id_type=MESH,
        )

    def bases(index, behind):
        base_x = atoms_ref[index, 4:5, :] + float(CX) * (-behind)
        base_z = atoms_ref[index, 6:7, :]
        coarse = jnp.floor(base_z * (1.0 / FINE))
        return base_x, atoms_ref[index, 5:6, :], coarse, base_z - coarse * FINE

    def prepare(index, behind):
        values, slopes = spline_tables(atoms_ref[index, 1:4, :])
        for offset in range(ORDER):
            slope_ref[index, offset, 0:3, :] = slopes[offset]
        base_x, base_y, coarse, rest = bases(index, behind)

        def rows(dim):
            return [value[dim : dim + 1] for value in values]

        plain_x = dense(base_x, rows(0), 8)
        dense_x_ref[index, 0] = plain_x
        dense_x_ref[index, 2] = atoms_ref[index, 0:1, :] * plain_x
        dense_y_ref[index, 0] = dense(base_y, rows(1), PATCH_Y)
        hit = lax.broadcasted_iota(jnp.int32, (COARSE, SLOTS), 0).astype(FLOAT) == coarse
        hit = jnp.where(hit, 1.0, 0.0).astype(HIGH_TYPE)
        fine_high, fine_low = split(dense(rest, rows(2), FAN))
        joined = jnp.concatenate([fine_high, fine_low, fine_high, hit, hit], axis=0)
        parts = dot(table_z_ref[: 4 * CZ], joined)
        cosine, sine = parts[:CZ], parts[CZ : 2 * CZ]
        turn_ref[index, :CZ] = cosine
        turn_ref[index, CZ:] = sine
        wave = cosine * parts[2 * CZ : 3 * CZ] + sine * parts[3 * CZ :]
        wave_high, wave_low = split(wave)
        z_ref[index, 0:CZ] = wave_high
        z_ref[index, CZ : 2 * CZ] = wave_low

    def prepare_slopes(index, behind):
        base_x, base_y, coarse, rest = bases(index, behind)

        def rows(dim):
            return [slope_ref[index, offset, dim : dim + 1, :] for offset in range(ORDER)]

        dense_x_ref[index, 1] = dense(base_x, rows(0), 8)
        dense_y_ref[index, 1] = dense(base_y, rows(1), PATCH_Y)
        high, low = split(dense(rest, rows(2), FAN))
        joined = jnp.concatenate([high, low, high], axis=0)
        parts = dot(table_z_ref[2 * CZ : 4 * CZ, : 3 * FAN], joined)
        wave = turn_ref[index, :CZ] * parts[:CZ] + turn_ref[index, CZ:] * parts[CZ:]
        high, low = split(wave)
        z_ref[index, 2 * CZ : 3 * CZ] = high
        z_ref[index, 3 * CZ :] = low

    def block(member):
        here, behind, part = member
        return here * 2 * COLS + behind * COLS + part

    def spread(member):
        index = block(member)
        here, _, part = member
        plain_y = dense_y_ref[index, 0]
        patch = jnp.concatenate(
            [dense_x_ref[index, 2, x : x + 1, :] * plain_y for x in range(CX)], axis=0
        )
        high, low = split(patch)
        both = dot(high, z_ref[index, 0 : 2 * CZ], True)
        summed = both[:, :CZ] + both[:, CZ:] + dot(low, z_ref[index, 0:CZ], True)
        rows = pl.ds(pl.multiple_of(part * CY, CY), PATCH_Y)
        for x in range(CX):
            acc_ref[here * CX + x, rows, :] += summed[x * PATCH_Y : (x + 1) * PATCH_Y]

    away = 1 - side
    near = [(away, 0, col), (side, 0, sibling), (away, 0, sibling)]
    near += [(here, 1, part) for here in (side, away) for part in (col, sibling)]
    far = [
        (here, behind, part) for here in (side, away) for behind in range(2) for part in far_cols
    ]
    fetches[0].wait()
    prepare(own, 0)
    pl.semaphore_wait(barrier, 3 + 4 * 5 + SIDE - 1)

    for group, parts in ((0, far_cols), (1, [sibling, col])):
        for other in parts:
            for behind, device_row in enumerate((row, row_after)):
                slot_at = (device_row // SIDE) * 2 * COLS + behind * COLS + col
                for target in (device_row, across(device_row)):
                    if other is col and target is row:
                        continue
                    remote(
                        atoms_ref.at[own],
                        atoms_ref.at[slot_at],
                        send_sems.at[0],
                        atoms_sems.at[group],
                        target,
                        other,
                    ).start()
    spread((side, 0, col))
    depth = SIDE * PART
    send_flat = send_ref.reshape(HALVES, SIDES, CX, depth, CZ)

    def arrive(group, count):
        remote(
            atoms_ref.at[0:count],
            atoms_ref.at[0:count],
            send_sems.at[0],
            atoms_sems.at[group],
            row_after,
            col,
        ).wait_recv()

    def work(members):
        for member in members:
            prepare(block(member), member[1])
        for member in members:
            spread(member)

    arrive(1, len(near))
    work(near)
    arrive(0, len(far))
    for here in (away, side):
        work([member for member in far if member[0] is here])
        if here is away:
            fetches[1].wait()
        for x in range(CX):
            acc_ref[here * CX + x, 0:8, :] += acc_ref[here * CX + x, KY : KY + 8, :]
        field = split(jnp.concatenate([acc_ref[here * CX + x, :KY] for x in range(CX)], axis=1))
        for half in range(HALVES):
            rows = slice(half * depth, (half + 1) * depth)
            result = dot3(table_y_ref[0, rows], table_y_ref[1, rows], *field)
            for x in range(CX):
                send_flat[half, here, x] = result[:, x * CZ : (x + 1) * CZ]

            @pl.loop(1, SIDE)
            def _(step):
                target = lax.rem(place + step, SIDE)
                remote(
                    send_ref.at[half, here, :, target],
                    turned_ref.at[half, here, place],
                    send_sems.at[1],
                    turned_sems.at[half],
                    side * SIDE + target,
                    col,
                ).start()

    for half in range(HALVES):
        turned_ref[half, :, place] = send_ref[half, :, :, place]

    for member in far + near:
        if member[0] is away:
            prepare_slopes(block(member), member[1])
    fetches[2].wait()
    fetches[3].wait()
    back_flat = back_ref.reshape(HALVES, KX * PART, CZ)
    turned_flat = turned_ref.reshape(HALVES, KX * PART, CZ)
    for half in range(HALVES):
        influence = jnp.concatenate(
            [
                influence_ref[pl.ds(half * PART + j, KX, stride=WIDTH), :]
                for j in range(PART)
            ],
            axis=1,
        )
        remote(
            turned_ref.at[half, :, 0 : SIDE - 1],
            turned_ref.at[half, :, 0 : SIDE - 1],
            send_sems.at[1],
            turned_sems.at[half],
            row_after,
            col,
        ).wait_recv()
        field = jnp.concatenate(
            [turned_flat[half, pl.ds(j, KX, stride=PART), :] for j in range(PART)], axis=1
        )
        high, low = split(field)
        spectrum = influence * dot3(table_x_ref[0, :KX], table_x_ref[1, :KX], high, low)
        high, low = split(spectrum)
        if half < HALVES - 1:
            pieces = [(slice(0, SIDES), 0, KX)]
        else:
            pieces = [(here, here * (KX // SIDES), KX // SIDES) for here in (away, side)]
        for number, (here, start, rows) in enumerate(pieces):
            if half < HALVES - 1:
                lines = pl.ds(0, KX)
            else:
                lines = pl.ds(pl.multiple_of(start, KX // SIDES), rows)
            result = dot3(table_x_ref[0, lines], table_x_ref[1, lines], high, low)
            for j in range(PART):
                back_flat[half, pl.ds(start * PART + j, rows, stride=PART), :] = result[
                    :, j * CZ : (j + 1) * CZ
                ]

            @pl.loop(1, SIDE)
            def _(step):
                target = lax.rem(place + step, SIDE)
                remote(
                    back_ref.at[half, here, target],
                    returned_ref.at[half, here, :, place],
                    send_sems.at[2],
                    returned_sems.at[half + number],
                    side * SIDE + target,
                    col,
                ).start()

        returned_ref[half, :, :, place] = back_ref[half, :, place]

    for member in far + near + [(side, 0, col)]:
        if member[0] is side:
            prepare_slopes(block(member), member[1])
    fetches[4].wait()

    def returned(half, here, number):
        remote(
            returned_ref.at[half, here, :, 0 : SIDE - 1],
            returned_ref.at[half, here, :, 0 : SIDE - 1],
            send_sems.at[2],
            returned_sems.at[number],
            row_after,
            col,
        ).wait_recv()

    for half in range(HALVES - 1):
        returned(half, slice(0, SIDES), half)
    returned_flat = returned_ref.reshape(HALVES, SIDES, CX, depth, CZ)
    mine = (side, 0, col)

    def collect(number, here):
        returned(HALVES - 1, here, HALVES - 1 + number)
        field = jnp.concatenate(
            [
                jnp.concatenate([returned_flat[half, here, x] for half in range(HALVES)], axis=0)
                for x in range(CX)
            ],
            axis=1,
        )
        high, low = split(field)
        result = dot3(table_back_ref[0], table_back_ref[1], high, low)
        for x in range(CX):
            acc_ref[here * CX + x] = result[:, x * CZ : (x + 1) * CZ]
    def contribute(member):
        here, behind, part = member
        index = block(member)
        plain_y = dense_y_ref[index, 0]
        slope_y = dense_y_ref[index, 1]
        rows = pl.ds(pl.multiple_of(part * CY, CY), PATCH_Y)
        patch = jnp.concatenate([acc_ref[here * CX + x, rows, :] for x in range(CX)], axis=0)
        high, low = split(patch)
        both = jnp.concatenate([high, low], axis=1)

        def contract(place_at):
            wave_high = z_ref[index, place_at * CZ : (place_at + 1) * CZ]
            wave_low = z_ref[index, (place_at + 1) * CZ : (place_at + 2) * CZ]
            twice = jnp.concatenate([wave_high, wave_high], axis=0)
            return dot(both, twice) + dot(high, wave_low)

        plain = contract(0)
        third = contract(2)
        sums = [0.0] * 4
        for x in range(CX):
            first_part = plain[x * PATCH_Y : (x + 1) * PATCH_Y]
            third_part = third[x * PATCH_Y : (x + 1) * PATCH_Y]
            inner = jnp.sum(plain_y * first_part, axis=0, keepdims=True)
            along_y = jnp.sum(slope_y * first_part, axis=0, keepdims=True)
            along_z = jnp.sum(plain_y * third_part, axis=0, keepdims=True)
            plain_x = dense_x_ref[index, 0, x : x + 1, :]
            slope_x = dense_x_ref[index, 1, x : x + 1, :]
            sums[0] = sums[0] + plain_x * inner
            sums[1] = sums[1] + slope_x * inner
            sums[2] = sums[2] + plain_x * along_y
            sums[3] = sums[3] + plain_x * along_z
        for k in range(4):
            partial_ref[index, k : k + 1] = sums[k]
        if member is not mine:
            remote(
                partial_ref.at[index],
                arrived_ref.at[behind * SIDES * COLS + side * COLS + col],
                send_sems.at[3],
                arrived_sem,
                lax.rem(here * SIDE + place + ROWS - behind, ROWS),
                part,
            ).start()

    for number, here in enumerate((away, side)):
        collect(number, here)
        members = [member for member in far + near if member[0] is here]
        if here is side:
            members.append(mine)
        for member in members:
            contribute(member)

    arrived_ref[side * COLS + col] = partial_ref[own]
    remote(
        arrived_ref.at[0 : BLOCKS - 1],
        arrived_ref.at[0 : BLOCKS - 1],
        send_sems.at[3],
        arrived_sem,
        row_after,
        col,
    ).wait()
    total = arrived_ref[0]
    for index in range(1, BLOCKS):
        total = total + arrived_ref[index]
    out_ref[...] = total
    remote(
        atoms_ref.at[0 : BLOCKS - 1],
        atoms_ref.at[0 : BLOCKS - 1],
        send_sems.at[0],
        atoms_sems.at[0],
        row_after,
        col,
    ).wait_send()
    remote(
        turned_ref.at[:, :, 0 : SIDE - 1],
        turned_ref.at[:, :, 0 : SIDE - 1],
        send_sems.at[1],
        turned_sems.at[0],
        row_after,
        col,
    ).wait_send()
    remote(
        returned_ref.at[:, :, :, 0 : SIDE - 1],
        returned_ref.at[:, :, :, 0 : SIDE - 1],
        send_sems.at[2],
        returned_sems.at[0],
        row_after,
        col,
    ).wait_send()


def finish_kernel(total_ref, charges_ref, counts_ref, out_charges_ref, out_coords_ref):
    slot = lax.broadcasted_iota(jnp.int32, (1, SLOTS), 1)
    live = slot < counts_ref[0]
    out_charges_ref[...] = jnp.where(live, total_ref[0:1], 0.0)
    out_coords_ref[...] = jnp.where(live, charges_ref[...], 0.0) * total_ref[1:4]


def shape(dims, kind=FLOAT):
    return jax.ShapeDtypeStruct(dims, kind)


def per_device(charges, fractions, base_cells, counts, influence):
    tables = [jnp.asarray(t) for t in make_tables()]
    anywhere = pl.BlockSpec(memory_space=pltpu.HBM)
    vector = pl.BlockSpec(memory_space=pltpu.VMEM)
    scalar = pl.BlockSpec(memory_space=pltpu.SMEM)
    dma = pltpu.SemaphoreType.DMA
    charges = charges.reshape(1, SLOTS)
    total = pl.pallas_call(
        kernel,
        out_shape=shape((4, SLOTS)),
        in_specs=[vector, vector, vector, scalar] + [anywhere] * 5,
        out_specs=vector,
        scratch_shapes=[
            pltpu.VMEM((KX * WIDTH, CZ), FLOAT),
            pltpu.VMEM(tables[0].shape, HIGH_TYPE),
            pltpu.VMEM(tables[1].shape[1:], HIGH_TYPE),
            pltpu.VMEM(tables[2].shape[1:], HIGH_TYPE),
            pltpu.VMEM(tables[3].shape[1:], HIGH_TYPE),
            pltpu.VMEM((BLOCKS, 8, SLOTS), FLOAT),
            pltpu.VMEM((BLOCKS, ORDER, 8, SLOTS), FLOAT),
            pltpu.VMEM((BLOCKS, 3, 8, SLOTS), FLOAT),
            pltpu.VMEM((BLOCKS, 2, PATCH_Y, SLOTS), FLOAT),
            pltpu.VMEM((BLOCKS, 4 * CZ, SLOTS), HIGH_TYPE),
            pltpu.VMEM((BLOCKS, 2 * CZ, SLOTS), FLOAT),
            pltpu.VMEM((SIDES * CX, KY + 8, CZ), FLOAT),
            pltpu.VMEM((HALVES, SIDES, CX, SIDE, PART, CZ), FLOAT),
            pltpu.VMEM((HALVES, SIDES, SIDE, CX, PART, CZ), FLOAT),
            pltpu.VMEM((HALVES, SIDES, SIDE, CX, PART, CZ), FLOAT),
            pltpu.VMEM((HALVES, SIDES, CX, SIDE, PART, CZ), FLOAT),
            pltpu.VMEM((BLOCKS, 4, SLOTS), FLOAT),
            pltpu.VMEM((BLOCKS, 4, SLOTS), FLOAT),
            dma((5,)),
            dma((4,)),
            dma((2,)),
            dma((HALVES,)),
            dma((HALVES + SIDES - 1,)),
            dma,
        ],
        compiler_params=pltpu.CompilerParams(
            collective_id=0, has_side_effects=True, vmem_limit_bytes=VMEM_LIMIT
        ),
    )(charges, fractions, base_cells, counts, influence.reshape(KX * WIDTH, CZ), *tables)
    grad_charges, grad_coords = pl.pallas_call(
        finish_kernel,
        out_shape=(shape((1, SLOTS)), shape((3, SLOTS))),
        in_specs=[vector, vector, scalar],
        out_specs=(vector, vector),
        compiler_params=pltpu.CompilerParams(vmem_limit_bytes=VMEM_LIMIT),
    )(total, charges, counts)
    return grad_charges.reshape(SLOTS), grad_coords


def solution(mesh):
    return jax.shard_map(
        per_device,
        mesh=mesh,
        in_specs=(
            P(("row", "col")),
            P(None, ("row", "col")),
            P(None, ("row", "col")),
            P(("row", "col")),
            P(None, "row", "col"),
        ),
        out_specs=(P(("row", "col")), P(None, ("row", "col"))),
        check_vma=False,
    )
```

```python
import math

import jax
import jax.numpy as jnp
import ml_dtypes
import numpy as np
from jax import lax
from jax.experimental import pallas as pl
from jax.experimental.pallas import tpu as pltpu
from jax.sharding import PartitionSpec as P

KX = 384
KY = 256
KZ = 512
ORDER = 6
SLOTS = 512
ROWS = 64
COLS = 4
CX = KX // ROWS
CY = KY // COLS
CZ = KZ // COLS
PATCH_Y = 72
FINE = 8
COARSE = KZ // FINE
FAN = 2 * FINE
VMEM_LIMIT = 63 * 1024 * 1024
HALVES = 1
WIDTH = KY // ROWS
PART = WIDTH // HALVES
SIDES = 2
SIDE = ROWS // SIDES
BLOCKS = 2 * SIDES * COLS
MESH = pl.DeviceIdType.MESH

HIGH_TYPE = jnp.bfloat16
FLOAT = jnp.float32


def split_table(table):
    high = table.astype(np.float32).astype(ml_dtypes.bfloat16)
    low = (table - high.astype(np.float64)).astype(np.float32).astype(ml_dtypes.bfloat16)
    return high, low


def cas(product, length):
    angles = (product % length) * (2.0 * math.pi / length)
    return np.cos(angles) + np.sin(angles)


def make_tables():
    kx = np.arange(KX)
    table_x = np.zeros((2, KX + 8, KX), ml_dtypes.bfloat16)
    table_x[:, :KX] = split_table(cas(kx[:, None] * kx[None, :], KX))
    ky = np.arange(KY).reshape(SIDES, SIDE, HALVES, PART).transpose(0, 2, 1, 3)
    ky = ky.reshape(SIDES, KY // SIDES)
    y = np.arange(KY + 8)
    table_y = np.stack(split_table(cas(ky[:, :, None] * np.arange(KY), KY)), axis=1)
    table_y = np.pad(table_y, ((0, 0), (0, 0), (0, 8), (0, 0)))
    table_back = np.stack(split_table(cas(y[None, :, None] * ky[:, None, :], KY)), axis=1)
    kz = np.arange(KZ)
    coarse = (kz[:, None] * np.arange(COARSE)[None, :] * FINE % KZ) * (2.0 * math.pi / KZ)
    fine = kz[:, None] * np.arange(FAN)[None, :]
    table_z = np.zeros((COLS, 4 * CZ, 3 * FAN + 2 * COARSE), ml_dtypes.bfloat16)
    for place, values in ((0, np.cos(coarse)), (1, np.sin(coarse))):
        high, low = split_table(values)
        rows = slice(place * CZ, (place + 1) * CZ)
        table_z[:, rows, 3 * FAN : 3 * FAN + COARSE] = high.reshape(COLS, CZ, COARSE)
        table_z[:, rows, 3 * FAN + COARSE :] = low.reshape(COLS, CZ, COARSE)
    for place, values in ((2, cas(fine, KZ)), (3, cas(-fine, KZ))):
        high, low = split_table(values)
        rows = slice(place * CZ, (place + 1) * CZ)
        table_z[:, rows, :FAN] = high.reshape(COLS, CZ, FAN)
        table_z[:, rows, FAN : 2 * FAN] = high.reshape(COLS, CZ, FAN)
        table_z[:, rows, 2 * FAN : 3 * FAN] = low.reshape(COLS, CZ, FAN)
    return table_x, table_y, table_back, np.pad(table_z, ((0, 0), (0, 8), (0, 0)))


def spline_tables(fraction):
    previous = [fraction, 1.0 - fraction]
    fifth_order = previous
    for degree in range(3, 7):
        current = []
        for position in range(degree):
            summed = None
            if position < degree - 1:
                summed = (fraction + position) * previous[position]
            if position >= 1:
                second = (degree - fraction - position) * previous[position - 1]
                summed = second if summed is None else summed + second
            current.append(summed * (1.0 / (degree - 1)))
        fifth_order = previous
        previous = current
    slopes = []
    for position in range(6):
        if position == 0:
            slopes.append(fifth_order[0])
        elif position == 5:
            slopes.append(-fifth_order[4])
        else:
            slopes.append(fifth_order[position] - fifth_order[position - 1])
    return previous[::-1], slopes[::-1]


def split(value):
    high = value.astype(HIGH_TYPE)
    return high, (value - high.astype(FLOAT)).astype(HIGH_TYPE)


def dot(left, right, transposed=False):
    dims = (((1,), (1 if transposed else 0,)), ((), ()))
    return lax.dot_general(left, right, dims, preferred_element_type=FLOAT)


def dot3(left_high, left_low, right_high, right_low):
    return (
        dot(left_high, right_high) + dot(left_high, right_low) + dot(left_low, right_high)
    )


def dense(base, weights, rows):
    distance = lax.broadcasted_iota(jnp.int32, (rows, SLOTS), 0).astype(FLOAT) - base
    total = jnp.zeros((rows, SLOTS), FLOAT)
    for offset in range(ORDER):
        total = jnp.where(distance == offset, weights[offset], total)
    return total


def kernel(
    charges_ref,
    fractions_ref,
    cells_ref,
    counts_ref,
    influence_hbm,
    table_x_hbm,
    table_y_hbm,
    table_back_hbm,
    table_z_hbm,
    out_ref,
    influence_ref,
    table_x_ref,
    table_y_ref,
    table_back_ref,
    table_z_ref,
    atoms_ref,
    slope_ref,
    dense_x_ref,
    dense_y_ref,
    z_ref,
    turn_ref,
    acc_ref,
    send_ref,
    turned_ref,
    back_ref,
    returned_ref,
    partial_ref,
    arrived_ref,
    local_sems,
    send_sems,
    atoms_sems,
    turned_sems,
    returned_sems,
    arrived_sem,
):
    row = lax.axis_index("row")
    col = lax.axis_index("col")
    half_at = col // 2
    core = lax.rem(col, 2)
    side = row // SIDE
    place = lax.rem(row, SIDE)
    row_after = lax.rem(row + 1, ROWS)
    row_before = lax.rem(row + ROWS - 1, ROWS)

    def across(device_row):
        return lax.rem(device_row + SIDE, ROWS)

    sibling = half_at * 2 + 1 - core
    far_cols = [(1 - half_at) * 2 + core, (1 - half_at) * 2 + 1 - core]

    barrier = pltpu.get_barrier_semaphore()

    def greet(device_row, device_col):
        pl.semaphore_signal(
            barrier, inc=1, device_id=(device_row, device_col), device_id_type=MESH
        )

    others = [across(row)]
    for device_row in (row_after, row_before):
        others += [device_row, across(device_row)]
    for other in far_cols + [sibling]:
        greet(row, other)
    for other in far_cols + [sibling, col]:
        for device_row in others:
            greet(device_row, other)

    @pl.loop(1, SIDE)
    def _(step):
        greet(side * SIDE + lax.rem(place + step, SIDE), col)

    fetches = [
        pltpu.make_async_copy(table_z_hbm.at[col], table_z_ref, local_sems.at[0]),
        pltpu.make_async_copy(table_y_hbm.at[side], table_y_ref, local_sems.at[1]),
        pltpu.make_async_copy(table_x_hbm, table_x_ref, local_sems.at[2]),
        pltpu.make_async_copy(influence_hbm, influence_ref, local_sems.at[3]),
        pltpu.make_async_copy(table_back_hbm.at[side], table_back_ref, local_sems.at[4]),
    ]
    for fetch in fetches:
        fetch.start()

    slot = lax.broadcasted_iota(jnp.int32, (1, SLOTS), 1)
    own = side * 2 * COLS + col
    weight = jnp.where(slot < counts_ref[0], charges_ref[...], 0.0)
    atoms_ref[own, 0:1, :] = weight
    atoms_ref[own, 1:4, :] = fractions_ref[...]
    cells = cells_ref[...]
    atoms_ref[own, 4:5, :] = (cells[0:1] - row * CX).astype(FLOAT)
    atoms_ref[own, 5:6, :] = (cells[1:2] - col * CY).astype(FLOAT)
    atoms_ref[own, 6:7, :] = cells[2:3].astype(FLOAT)
    atoms_ref[own, 7:8, :] = weight
    acc_ref[...] = jnp.zeros(acc_ref.shape, FLOAT)

    def remote(source, target, send_sem, recv_sem, device_row, device_col):
        return pltpu.make_async_remote_copy(
            src_ref=source,
            dst_ref=target,
            send_sem=send_sem,
            recv_sem=recv_sem,
            device_id=(device_row, device_col),
            device_id_type=MESH,
        )

    def bases(index, behind):
        base_x = atoms_ref[index, 4:5, :] + float(CX) * (-behind)
        base_z = atoms_ref[index, 6:7, :]
        coarse = jnp.floor(base_z * (1.0 / FINE))
        return base_x, atoms_ref[index, 5:6, :], coarse, base_z - coarse * FINE

    def prepare(index, behind):
        values, slopes = spline_tables(atoms_ref[index, 1:4, :])
        for offset in range(ORDER):
            slope_ref[index, offset, 0:3, :] = slopes[offset]
        base_x, base_y, coarse, rest = bases(index, behind)

        def rows(dim):
            return [value[dim : dim + 1] for value in values]

        plain_x = dense(base_x, rows(0), 8)
        dense_x_ref[index, 0] = plain_x
        dense_x_ref[index, 2] = atoms_ref[index, 0:1, :] * plain_x
        dense_y_ref[index, 0] = dense(base_y, rows(1), PATCH_Y)
        hit = lax.broadcasted_iota(jnp.int32, (COARSE, SLOTS), 0).astype(FLOAT) == coarse
        hit = jnp.where(hit, 1.0, 0.0).astype(HIGH_TYPE)
        fine_high, fine_low = split(dense(rest, rows(2), FAN))
        joined = jnp.concatenate([fine_high, fine_low, fine_high, hit, hit], axis=0)
        parts = dot(table_z_ref[: 4 * CZ], joined)
        cosine, sine = parts[:CZ], parts[CZ : 2 * CZ]
        turn_ref[index, :CZ] = cosine
        turn_ref[index, CZ:] = sine
        wave = cosine * parts[2 * CZ : 3 * CZ] + sine * parts[3 * CZ :]
        wave_high, wave_low = split(wave)
        z_ref[index, 0:CZ] = wave_high
        z_ref[index, CZ : 2 * CZ] = wave_low

    def prepare_slopes(index, behind):
        base_x, base_y, coarse, rest = bases(index, behind)

        def rows(dim):
            return [slope_ref[index, offset, dim : dim + 1, :] for offset in range(ORDER)]

        dense_x_ref[index, 1] = dense(base_x, rows(0), 8)
        dense_y_ref[index, 1] = dense(base_y, rows(1), PATCH_Y)
        high, low = split(dense(rest, rows(2), FAN))
        joined = jnp.concatenate([high, low, high], axis=0)
        parts = dot(table_z_ref[2 * CZ : 4 * CZ, : 3 * FAN], joined)
        wave = turn_ref[index, :CZ] * parts[:CZ] + turn_ref[index, CZ:] * parts[CZ:]
        high, low = split(wave)
        z_ref[index, 2 * CZ : 3 * CZ] = high
        z_ref[index, 3 * CZ :] = low

    def block(member):
        here, behind, part = member
        return here * 2 * COLS + behind * COLS + part

    def spread(member):
        index = block(member)
        here, _, part = member
        plain_y = dense_y_ref[index, 0]
        patch = jnp.concatenate(
            [dense_x_ref[index, 2, x : x + 1, :] * plain_y for x in range(CX)], axis=0
        )
        high, low = split(patch)
        both = dot(high, z_ref[index, 0 : 2 * CZ], True)
        summed = both[:, :CZ] + both[:, CZ:] + dot(low, z_ref[index, 0:CZ], True)
        rows = pl.ds(pl.multiple_of(part * CY, CY), PATCH_Y)
        for x in range(CX):
            acc_ref[here * CX + x, rows, :] += summed[x * PATCH_Y : (x + 1) * PATCH_Y]

    away = 1 - side
    near = [(away, 0, col), (side, 0, sibling), (away, 0, sibling)]
    near += [(here, 1, part) for here in (side, away) for part in (col, sibling)]
    far = [
        (here, behind, part) for here in (side, away) for behind in range(2) for part in far_cols
    ]
    fetches[0].wait()
    prepare(own, 0)
    pl.semaphore_wait(barrier, 3 + 4 * 5 + SIDE - 1)

    for group, parts in ((0, far_cols), (1, [sibling, col])):
        for other in parts:
            for behind, device_row in enumerate((row, row_after)):
                slot_at = (device_row // SIDE) * 2 * COLS + behind * COLS + col
                for target in (device_row, across(device_row)):
                    if other is col and target is row:
                        continue
                    remote(
                        atoms_ref.at[own],
                        atoms_ref.at[slot_at],
                        send_sems.at[0],
                        atoms_sems.at[group],
                        target,
                        other,
                    ).start()
    spread((side, 0, col))
    depth = SIDE * PART
    send_flat = send_ref.reshape(HALVES, SIDES, CX, depth, CZ)

    def arrive(group, count):
        remote(
            atoms_ref.at[0:count],
            atoms_ref.at[0:count],
            send_sems.at[0],
            atoms_sems.at[group],
            row_after,
            col,
        ).wait_recv()

    def work(members):
        for member in members:
            prepare(block(member), member[1])
        for member in members:
            spread(member)

    arrive(1, len(near))
    work(near)
    arrive(0, len(far))
    for here in (away, side):
        work([member for member in far if member[0] is here])
        if here is away:
            fetches[1].wait()
        for x in range(CX):
            acc_ref[here * CX + x, 0:8, :] += acc_ref[here * CX + x, KY : KY + 8, :]
        field = split(jnp.concatenate([acc_ref[here * CX + x, :KY] for x in range(CX)], axis=1))
        for half in range(HALVES):
            rows = slice(half * depth, (half + 1) * depth)
            result = dot3(table_y_ref[0, rows], table_y_ref[1, rows], *field)
            for x in range(CX):
                send_flat[half, here, x] = result[:, x * CZ : (x + 1) * CZ]

            @pl.loop(1, SIDE)
            def _(step):
                target = lax.rem(place + step, SIDE)
                remote(
                    send_ref.at[half, here, :, target],
                    turned_ref.at[half, here, place],
                    send_sems.at[1],
                    turned_sems.at[half],
                    side * SIDE + target,
                    col,
                ).start()

    for half in range(HALVES):
        turned_ref[half, :, place] = send_ref[half, :, :, place]

    for member in far + near + [(side, 0, col)]:
        prepare_slopes(block(member), member[1])
    fetches[2].wait()
    fetches[3].wait()
    back_flat = back_ref.reshape(HALVES, KX * PART, CZ)
    turned_flat = turned_ref.reshape(HALVES, KX * PART, CZ)
    for half in range(HALVES):
        influence = jnp.concatenate(
            [
                influence_ref[pl.ds(half * PART + j, KX, stride=WIDTH), :]
                for j in range(PART)
            ],
            axis=1,
        )
        remote(
            turned_ref.at[half, :, 0 : SIDE - 1],
            turned_ref.at[half, :, 0 : SIDE - 1],
            send_sems.at[1],
            turned_sems.at[half],
            row_after,
            col,
        ).wait_recv()
        field = jnp.concatenate(
            [turned_flat[half, pl.ds(j, KX, stride=PART), :] for j in range(PART)], axis=1
        )
        high, low = split(field)
        spectrum = influence * dot3(table_x_ref[0, :KX], table_x_ref[1, :KX], high, low)
        high, low = split(spectrum)
        result = dot3(table_x_ref[0, :KX], table_x_ref[1, :KX], high, low)
        for j in range(PART):
            back_flat[half, pl.ds(j, KX, stride=PART), :] = result[:, j * CZ : (j + 1) * CZ]

        if half < HALVES - 1:
            pieces = [slice(0, SIDES)]
        else:
            pieces = [away, side]
        for number, here in enumerate(pieces):

            @pl.loop(1, SIDE)
            def _(step):
                target = lax.rem(place + step, SIDE)
                source = back_ref.at[half, here, target]
                landing = returned_ref.at[half, here, :, place]
                remote(
                    source,
                    landing,
                    send_sems.at[2],
                    returned_sems.at[half + number],
                    side * SIDE + target,
                    col,
                ).start()

        returned_ref[half, :, :, place] = back_ref[half, :, place]

    fetches[4].wait()
    def returned(half, here, number):
        remote(
            returned_ref.at[half, here, :, 0 : SIDE - 1],
            returned_ref.at[half, here, :, 0 : SIDE - 1],
            send_sems.at[2],
            returned_sems.at[number],
            row_after,
            col,
        ).wait_recv()

    for half in range(HALVES - 1):
        returned(half, slice(0, SIDES), half)
    returned_flat = returned_ref.reshape(HALVES, SIDES, CX, depth, CZ)
    mine = (side, 0, col)

    def collect(number, here):
        returned(HALVES - 1, here, HALVES - 1 + number)
        field = jnp.concatenate(
            [
                jnp.concatenate([returned_flat[half, here, x] for half in range(HALVES)], axis=0)
                for x in range(CX)
            ],
            axis=1,
        )
        high, low = split(field)
        result = dot3(table_back_ref[0], table_back_ref[1], high, low)
        for x in range(CX):
            acc_ref[here * CX + x] = result[:, x * CZ : (x + 1) * CZ]
    def contribute(member):
        here, behind, part = member
        index = block(member)
        plain_y = dense_y_ref[index, 0]
        slope_y = dense_y_ref[index, 1]
        rows = pl.ds(pl.multiple_of(part * CY, CY), PATCH_Y)
        patch = jnp.concatenate([acc_ref[here * CX + x, rows, :] for x in range(CX)], axis=0)
        high, low = split(patch)
        both = jnp.concatenate([high, low], axis=1)

        def contract(place_at):
            wave_high = z_ref[index, place_at * CZ : (place_at + 1) * CZ]
            wave_low = z_ref[index, (place_at + 1) * CZ : (place_at + 2) * CZ]
            twice = jnp.concatenate([wave_high, wave_high], axis=0)
            return dot(both, twice) + dot(high, wave_low)

        plain = contract(0)
        third = contract(2)
        sums = [0.0] * 4
        for x in range(CX):
            first_part = plain[x * PATCH_Y : (x + 1) * PATCH_Y]
            third_part = third[x * PATCH_Y : (x + 1) * PATCH_Y]
            inner = jnp.sum(plain_y * first_part, axis=0, keepdims=True)
            along_y = jnp.sum(slope_y * first_part, axis=0, keepdims=True)
            along_z = jnp.sum(plain_y * third_part, axis=0, keepdims=True)
            plain_x = dense_x_ref[index, 0, x : x + 1, :]
            slope_x = dense_x_ref[index, 1, x : x + 1, :]
            sums[0] = sums[0] + plain_x * inner
            sums[1] = sums[1] + slope_x * inner
            sums[2] = sums[2] + plain_x * along_y
            sums[3] = sums[3] + plain_x * along_z
        for k in range(4):
            partial_ref[index, k : k + 1] = sums[k]
        if member is not mine:
            remote(
                partial_ref.at[index],
                arrived_ref.at[behind * SIDES * COLS + side * COLS + col],
                send_sems.at[3],
                arrived_sem,
                lax.rem(here * SIDE + place + ROWS - behind, ROWS),
                part,
            ).start()

    for number, here in enumerate((away, side)):
        collect(number, here)
        members = [member for member in far + near if member[0] is here]
        if here is side:
            members.append(mine)
        for member in members:
            contribute(member)

    arrived_ref[side * COLS + col] = partial_ref[own]
    remote(
        arrived_ref.at[0 : BLOCKS - 1],
        arrived_ref.at[0 : BLOCKS - 1],
        send_sems.at[3],
        arrived_sem,
        row_after,
        col,
    ).wait()
    total = arrived_ref[0]
    for index in range(1, BLOCKS):
        total = total + arrived_ref[index]
    out_ref[...] = total
    remote(
        atoms_ref.at[0 : BLOCKS - 1],
        atoms_ref.at[0 : BLOCKS - 1],
        send_sems.at[0],
        atoms_sems.at[0],
        row_after,
        col,
    ).wait_send()
    remote(
        turned_ref.at[:, :, 0 : SIDE - 1],
        turned_ref.at[:, :, 0 : SIDE - 1],
        send_sems.at[1],
        turned_sems.at[0],
        row_after,
        col,
    ).wait_send()
    remote(
        returned_ref.at[:, :, :, 0 : SIDE - 1],
        returned_ref.at[:, :, :, 0 : SIDE - 1],
        send_sems.at[2],
        returned_sems.at[0],
        row_after,
        col,
    ).wait_send()


def finish_kernel(total_ref, charges_ref, counts_ref, out_charges_ref, out_coords_ref):
    slot = lax.broadcasted_iota(jnp.int32, (1, SLOTS), 1)
    live = slot < counts_ref[0]
    out_charges_ref[...] = jnp.where(live, total_ref[0:1], 0.0)
    out_coords_ref[...] = jnp.where(live, charges_ref[...], 0.0) * total_ref[1:4]


def shape(dims, kind=FLOAT):
    return jax.ShapeDtypeStruct(dims, kind)


def per_device(charges, fractions, base_cells, counts, influence):
    tables = [jnp.asarray(t) for t in make_tables()]
    anywhere = pl.BlockSpec(memory_space=pltpu.HBM)
    vector = pl.BlockSpec(memory_space=pltpu.VMEM)
    scalar = pl.BlockSpec(memory_space=pltpu.SMEM)
    dma = pltpu.SemaphoreType.DMA
    charges = charges.reshape(1, SLOTS)
    total = pl.pallas_call(
        kernel,
        out_shape=shape((4, SLOTS)),
        in_specs=[vector, vector, vector, scalar] + [anywhere] * 5,
        out_specs=vector,
        scratch_shapes=[
            pltpu.VMEM((KX * WIDTH, CZ), FLOAT),
            pltpu.VMEM(tables[0].shape, HIGH_TYPE),
            pltpu.VMEM(tables[1].shape[1:], HIGH_TYPE),
            pltpu.VMEM(tables[2].shape[1:], HIGH_TYPE),
            pltpu.VMEM(tables[3].shape[1:], HIGH_TYPE),
            pltpu.VMEM((BLOCKS, 8, SLOTS), FLOAT),
            pltpu.VMEM((BLOCKS, ORDER, 8, SLOTS), FLOAT),
            pltpu.VMEM((BLOCKS, 3, 8, SLOTS), FLOAT),
            pltpu.VMEM((BLOCKS, 2, PATCH_Y, SLOTS), FLOAT),
            pltpu.VMEM((BLOCKS, 4 * CZ, SLOTS), HIGH_TYPE),
            pltpu.VMEM((BLOCKS, 2 * CZ, SLOTS), FLOAT),
            pltpu.VMEM((SIDES * CX, KY + 8, CZ), FLOAT),
            pltpu.VMEM((HALVES, SIDES, CX, SIDE, PART, CZ), FLOAT),
            pltpu.VMEM((HALVES, SIDES, SIDE, CX, PART, CZ), FLOAT),
            pltpu.VMEM((HALVES, SIDES, SIDE, CX, PART, CZ), FLOAT),
            pltpu.VMEM((HALVES, SIDES, CX, SIDE, PART, CZ), FLOAT),
            pltpu.VMEM((BLOCKS, 4, SLOTS), FLOAT),
            pltpu.VMEM((BLOCKS, 4, SLOTS), FLOAT),
            dma((5,)),
            dma((4,)),
            dma((2,)),
            dma((HALVES,)),
            dma((HALVES + SIDES - 1,)),
            dma,
        ],
        compiler_params=pltpu.CompilerParams(
            collective_id=0, has_side_effects=True, vmem_limit_bytes=VMEM_LIMIT
        ),
    )(charges, fractions, base_cells, counts, influence.reshape(KX * WIDTH, CZ), *tables)
    grad_charges, grad_coords = pl.pallas_call(
        finish_kernel,
        out_shape=(shape((1, SLOTS)), shape((3, SLOTS))),
        in_specs=[vector, vector, scalar],
        out_specs=(vector, vector),
        compiler_params=pltpu.CompilerParams(vmem_limit_bytes=VMEM_LIMIT),
    )(total, charges, counts)
    return grad_charges.reshape(SLOTS), grad_coords


def solution(mesh):
    return jax.shard_map(
        per_device,
        mesh=mesh,
        in_specs=(
            P(("row", "col")),
            P(None, ("row", "col")),
            P(None, ("row", "col")),
            P(("row", "col")),
            P(None, "row", "col"),
        ),
        out_specs=(P(("row", "col")), P(None, ("row", "col"))),
        check_vma=False,
    )
```
